512 devices in a mesh: row: 16 (over y, core), col: 32 (over z, x).
Axes of the slice: x: 4, y: 8, z: 8, core: 2. Of those that a mesh axis runs over, the one named last changes fastest.
Arguments:
- tokens: bfloat16 [512, 6144], P('col', 'row'), may hold values from -21 to 21
- token_frame: int32 [512], P('col'), may hold values from 0 to 15, never falling along the last dimension, each value on 1 to 64 neighbouring positions
- noise_level: int32 [16], replicated, may hold values from 0 to 63
- modulation: bfloat16 [64, 3, 6144], P(None, None, 'row'), may hold values from -3 to 3
- gate_weight: bfloat16 [6144, 16384], P('row', 'col'), may hold values from -0.078125 to 0.078125
- up_weight: bfloat16 [6144, 16384], P('row', 'col'), may hold values from -0.078125 to 0.078125
- down_weight: bfloat16 [16384, 6144], P('col', 'row'), may hold values from -0.046875 to 0.046875
Outputs:
- mixed: bfloat16 [512, 6144], P('col', 'row')
The draws below stay inside these ranges and needn't reach their ends.
Inputs may be any that keep to these rules, and one draw needn't show every extreme that they name: token_frame never falls along the tokens.
All inputs are finite; a program needn't handle non-finite values.
Results may differ from the reference program's by a relative error of at most 0.015.
Values may be sent and summed in bfloat16 or wider, within the bound.
A program may use at most 64 MiB of HBM per device.

```python
import math
import jax
import jax.numpy as jnp
import numpy as np
from jax import lax

D = 6144
FF = 16384
FRAMES = 16
LEVELS = 64
TOKENS = 512
N_ROW = 16
N_COL = 32


def draw_tokens(key, part):
    key = jax.random.fold_in(key, 7)
    first, second = jax.random.split(key, 2)
    column = jnp.arange(D, dtype=jnp.float32)
    rising = jnp.exp(math.log(3.0) * column / (D - 1)) * jax.random.uniform(second, (D,), minval=0.7, maxval=1.3)
    values = jnp.clip(jax.random.normal(first, (TOKENS, D)), -4.0, 4.0)
    result = values * rising[None, :] * 0.8
    return result.astype(jnp.bfloat16)


def plant(array, rng, smallest, top_value):
    longest = array.shape.index(max(array.shape))
    spots = []
    for shift in (0, 1):
        where = [jax.random.randint(jax.random.fold_in(rng, axis), (), 0, length) for axis, length in enumerate(array.shape)]
        where[longest] = (where[longest] + shift) % array.shape[longest]
        spots.append(tuple(where))
    return array.at[spots[0]].set(smallest).at[spots[1]].set(top_value)


def steps_of(stream_key, extent, pieces, least, high):
    def one(dim, blocks):
        steps = jax.random.uniform(jax.random.fold_in(jax.random.fold_in(stream_key, 6), dim), (blocks,), jnp.float32, least / len(pieces), high / len(pieces))
        return jnp.repeat(jnp.exp(steps), extent[dim] // blocks).reshape((-1,) + (1,) * (len(extent) - dim - 1))

    gain = one(*pieces[0])
    for cut in pieces[1:]:
        gain = gain * one(*cut)
    return gain


def profile(amount, total, limit, slope):
    weights = [(1 << 20) // math.isqrt(standing ** slope) + 1 for standing in range(2, amount + 1)]
    spare, counts = total - limit - (amount - 1), [1] * (amount - 1)
    while spare > 0:
        candidates = [i for i in range(amount - 1) if counts[i] < limit]
        pool, left = sum([weights[i] for i in candidates]), spare
        for i in candidates:
            more = min(limit - counts[i], max(1, left * weights[i] // pool), spare)
            counts[i] = counts[i] + more
            spare = spare - more
    return np.array([limit] + counts)


def uneven(own_key, number_of, total, reach, skew):
    if number_of == 2:
        one = jax.random.randint(own_key, (), max(1, total - reach), min(reach, total - 1) + 1)
        return jnp.stack([one, total - one])
    tallies = jnp.asarray(profile(number_of, total, reach, skew), jnp.int32)
    twos = (number_of - 1) // 2
    giver, receiver = tallies[1:1 + 2 * twos:2], tallies[2:2 + 2 * twos:2]
    slack = jnp.minimum(giver - 1, reach - receiver)
    shifted = jax.random.randint(jax.random.fold_in(own_key, 1), (twos,), 0, 1 << 20) % (slack + 1)
    tallies = tallies.at[1:1 + 2 * twos:2].set(giver - shifted).at[2:2 + 2 * twos:2].set(receiver + shifted)
    return tallies[jax.random.permutation(jax.random.fold_in(own_key, 2), number_of)]


def gaussian(rng, extent, scale, limit, pieces=(), kind=jnp.bfloat16):
    entries = scale * jax.random.normal(rng, extent, jnp.float32)
    if pieces:
        entries = entries * steps_of(rng, extent, pieces, -0.22, 0.18)
    return jnp.clip(entries, -limit, limit).astype(kind)


def setup_inputs(seed: int = 0) -> dict:
    key_of = jax.random.split(jax.random.key(seed), 8)
    tokens = draw_tokens(jax.random.fold_in(key_of[7], 71), 0)
    token_frame = jnp.searchsorted(jnp.cumsum(uneven(key_of[1], FRAMES, TOKENS, 2 * TOKENS // FRAMES, 1)), jnp.arange(TOKENS), side="right").astype(jnp.int32)
    noise_level = plant(jax.random.randint(key_of[2], (FRAMES,), 0, LEVELS), jax.random.fold_in(key_of[2], 1), 0, LEVELS - 1).astype(jnp.int32)
    modulation = gaussian(key_of[3], (LEVELS, 3, D), 0.5, 3.0, ((2, 16),))
    gate_weight = gaussian(key_of[4], (D, FF), D ** -0.5, 0.078125, ((0, 16), (1, 32)))
    up_weight = gaussian(key_of[5], (D, FF), D ** -0.5, 0.078125, ((0, 16), (1, 32)))
    down_weight = gaussian(key_of[6], (FF, D), FF ** -0.5, 0.046875, ((0, 32), (1, 16)))
    return dict(tokens=tokens, token_frame=token_frame, noise_level=noise_level, modulation=modulation, gate_weight=gate_weight, up_weight=up_weight, down_weight=down_weight)


epsilon = 1e-06

def blocked_product(left, right, parts):
    panel = left.shape[1] // parts
    total = jnp.zeros((left.shape[0], right.shape[1]), jnp.float32)
    for block in range(parts):
        term = jnp.dot(left[:, block * panel:(block + 1) * panel], right[block * panel:(block + 1) * panel], preferred_element_type=jnp.float32)
        rounded = lax.optimization_barrier(term.astype(jnp.bfloat16))
        total = total + rounded.astype(jnp.float32)
    return total

def reference(tokens, token_frame, noise_level, modulation, gate_weight, up_weight, down_weight):
    level = noise_level[token_frame]
    mods = modulation[level].astype(jnp.float32)
    wide_tokens = tokens.astype(jnp.float32)
    center = lax.optimization_barrier(jnp.mean(wide_tokens, axis=1))
    spread = lax.optimization_barrier(jnp.mean(wide_tokens * wide_tokens, axis=1)) - center * center
    normed = ((wide_tokens - center[:, None]) * lax.rsqrt(spread + epsilon)[:, None] * (1.0 + mods[:, 1]) + mods[:, 0]).astype(jnp.bfloat16)
    gate = blocked_product(normed, gate_weight, N_ROW)
    upper = blocked_product(normed, up_weight, N_ROW)
    hidden = (jax.nn.silu(gate) * upper).astype(jnp.bfloat16)
    branch = blocked_product(hidden, down_weight, N_COL)
    return (wide_tokens + mods[:, 2] * branch).astype(jnp.bfloat16)
```

```python
import jax
import jax.numpy as jnp
from jax import lax
from jax.experimental import pallas as pl
from jax.experimental.pallas import tpu as pltpu
from jax.sharding import PartitionSpec as P

D = 6144
EPS = 1e-06
NY, NZ, NX = 8, 8, 4
MESH = pl.DeviceIdType.MESH
F32, BF16 = jnp.float32, jnp.bfloat16


def place(y, core, z, x):
    return (y * 2 + core, z * NX + x)


def pieces(value):
    high = value.astype(BF16).astype(F32)
    rest = value - high
    middle = rest.astype(BF16).astype(F32)
    return high, middle, rest - middle


def in_lanes(lane, first, columns, base):
    for i, column in enumerate(columns):
        base = jnp.where(lane == first + i, column, base)
    return base


def send(src, dst, send_sem, recv_sem, device):
    pltpu.make_async_remote_copy(
        src, dst, send_sem, recv_sem, device_id=device, device_id_type=MESH
    ).start()


def await_bytes(ref, sem):
    pltpu.make_async_copy(ref, ref, sem).wait()


def kernel(
    tokens, frame, noise, modulation, gate_w, up_w, down_w, out,
    own, table, w1, w2, sum_out, sum_in, stat_out, stats, gathered, fields, picks,
    normed, part, part_in, hidden, down, down_in, down_mid, branch_in, own_out,
    local_sem, share_send, share_recv, sum_send, sum_recv, tok_send, tok_recv,
    fwd_send, fwd_recv, stat_send, stat_recv, statf_send, statf_recv, part_send, part_recv, hid_send, hid_recv,
    dx_send, dx_recv, dz_send, dz_recv, stat_recv_own,
):
    row, col = lax.axis_index("row"), lax.axis_index("col")
    y, k, z, x = row // 2, row % 2, col // NX, col % NX
    hz = z // 4
    zz = z % 4
    sibling = place(y, 1 - k, z, x)

    own_copy = pltpu.make_async_copy(tokens, own, local_sem.at[0])
    own_copy.start()
    local = [
        pltpu.make_async_copy(modulation, table.at[k], local_sem.at[1]),
        pltpu.make_async_copy(gate_w, w1.at[pl.ds(384 * k, 384), pl.ds(0, 512)], local_sem.at[2]),
        pltpu.make_async_copy(up_w, w1.at[pl.ds(384 * k, 384), pl.ds(512, 512)], local_sem.at[3]),
        pltpu.make_async_copy(down_w, w2.at[k], local_sem.at[4]),
    ]
    for copy in local:
        copy.start()

    barrier = pltpu.get_barrier_semaphore()
    peers = [place((y + dy) % NY, (k + dk) % 2, z, x) for dy in (4, 3, 5, 2, 6, 1, 7, 0) for dk in (0, 1) if dy or dk]
    peers += [place(y, (k + dk) % 2, (z + dz) % NZ, x) for dz in (4, 3, 5, 2, 6, 1, 7) for dk in (0, 1)]
    peers += [place(y, k, z, (x + dx) % NX) for dx in (2, 1, 3)]
    for peer in peers:
        pl.semaphore_signal(barrier, inc=1, device_id=peer, device_id_type=MESH)

    own_copy.wait()
    wide = own[...].astype(F32)
    lane = lax.broadcasted_iota(jnp.int32, (16, 128), 1)
    sublane = lax.broadcasted_iota(jnp.int32, (16, 128), 0)
    zero = jnp.zeros((16, 128), F32)
    columns = pieces(jnp.sum(wide, axis=1, keepdims=True)) + pieces(jnp.sum(wide * wide, axis=1, keepdims=True))
    sums = in_lanes(lane, 0, columns, zero).astype(BF16)
    sum_out[...] = sums
    sum_in[row] = sums
    onehot = zero
    for t in range(16):
        level = noise[frame[t]]
        onehot = jnp.where((sublane == t) & (lane == level), 1.0, onehot)

    pl.semaphore_wait(barrier, len(peers))

    for dy in (4, 3, 5, 2, 6, 1, 7, 0):
        for dk in (0, 1):
            if dy or dk:
                send(sum_out, sum_in.at[row], sum_send, sum_recv, place((y + dy) % NY, (k + dk) % 2, z, x))
    block = pl.ds(64 * zz + 16 * x, 16)
    for dz in (4, 3, 5, 2, 6, 1, 7):
        send(own, gathered.at[k, block], tok_send, tok_recv.at[zz, k], place(y, hz, (z + dz) % NZ, x))

    @pl.when(k == hz)
    def _():
        pltpu.make_async_copy(own, gathered.at[k, block], tok_recv.at[zz, k]).start()

    @pl.when(k != hz)
    def _():
        send(own, gathered.at[k, block], tok_send, tok_recv.at[zz, k], sibling)

    send(modulation, table.at[k], share_send.at[0], share_recv.at[0], sibling)
    send(gate_w, w1.at[pl.ds(384 * k, 384), pl.ds(0, 512)], share_send.at[1], share_recv.at[1], sibling)
    send(up_w, w1.at[pl.ds(384 * k, 384), pl.ds(512, 512)], share_send.at[2], share_recv.at[2], sibling)
    send(down_w, w2.at[k], share_send.at[3], share_recv.at[3], sibling)

    await_bytes(sum_in.at[pl.ds(0, 15)], sum_recv)
    total = jnp.sum(sum_in[...].astype(F32), axis=0)
    center = jnp.sum(jnp.where(lane < 3, total, 0.0), axis=1, keepdims=True) / D
    square = jnp.sum(jnp.where((lane >= 3) & (lane < 6), total, 0.0), axis=1, keepdims=True) / D
    scale = lax.rsqrt(square - center * center + EPS)
    stat_out[...] = in_lanes(lane, 64, pieces(center) + pieces(scale), onehot).astype(BF16)

    @pl.when(k == hz)
    def _():
        for dz in (4, 3, 5, 2, 6, 1, 7):
            send(stat_out, stats.at[block], stat_send, stat_recv.at[zz], place(y, k, (z + dz) % NZ, x))
        pltpu.make_async_copy(stat_out, stats.at[block], stat_recv.at[zz]).start()

    for i in range(4):
        from_z = (zz + i) % 4
        came = pl.ds(64 * from_z + 16 * x, 16)
        for kk in (0, 1):
            await_bytes(gathered.at[kk, came], tok_recv.at[from_z, kk])
            for dx in (2, 1, 3):
                send(gathered.at[kk, came], gathered.at[kk, came], fwd_send, fwd_recv, place(y, k, z, (x + dx) % NX))

    local[0].wait()
    await_bytes(table.at[0], share_recv.at[0])
    for kk in (0, 1):
        fields[kk, 64:128, :] = jnp.zeros((64, 768), BF16)
        fields[kk, 0:64, 0:384] = table[kk, :, 0, :]
        fields[kk, 0:64, 384:768] = table[kk, :, 1, :]
    gate_mod = jnp.dot(onehot.astype(BF16)[:, 0:64], table[k, :, 2, :], preferred_element_type=F32)
    source = lax.broadcasted_iota(jnp.int32, (128, 256), 0)
    target = lax.broadcasted_iota(jnp.int32, (128, 256), 1)
    picks[...] = jnp.where(
        ((target < 128) & (source >= 64) & (source < 67)) | ((target >= 128) & (source >= 67) & (source < 70)), 1.0, 0.0
    ).astype(BF16)

    for i in range(4):
        from_z = (zz + i) % 4
        came = pl.ds(64 * from_z + 16 * x, 16)
        await_bytes(stats.at[came], stat_recv.at[from_z])
        for dx in (2, 1, 3):
            send(stats.at[came], stats.at[came], statf_send, statf_recv, place(y, k, z, (x + dx) % NX))
    await_bytes(gathered.at[:, pl.ds(0, 192)], fwd_recv)
    await_bytes(stats.at[pl.ds(0, 192)], statf_recv)

    table_of = stats[...]
    moments = jnp.dot(table_of, picks[...], preferred_element_type=F32)
    for kk in (0, 1):
        mods = jnp.dot(table_of, fields[kk], preferred_element_type=F32)
        for part_of in range(3):
            at = slice(128 * part_of, 128 * part_of + 128)
            after = slice(384 + 128 * part_of, 512 + 128 * part_of)
            normed[:, 384 * kk + 128 * part_of : 384 * kk + 128 * part_of + 128] = (
                (gathered[kk, :, at].astype(F32) - moments[:, 0:128]) * moments[:, 128:256] * (1.0 + mods[:, after])
                + mods[:, at]
            ).astype(BF16)

    local[1].wait()
    local[2].wait()
    await_bytes(w1.at[pl.ds(0, 384), pl.ds(0, 512)], share_recv.at[1])
    await_bytes(w1.at[pl.ds(0, 384), pl.ds(0, 512)], share_recv.at[2])
    for n in range(2):
        at = slice(512 * n, 512 * n + 512)
        part[:, at] = jnp.dot(normed[...], w1[:, at], preferred_element_type=F32).astype(BF16)
    for dy in (4, 3, 5, 2, 6, 1, 7):
        to = (y + dy) % NY
        send(part.at[pl.ds(32 * to, 32)], part_in.at[dy - 1], part_send, part_recv, place(to, k, z, x))

    await_bytes(sum_in.at[pl.ds(0, 15)], sum_send)
    await_bytes(gathered.at[0, pl.ds(0, 112)], tok_send)

    @pl.when(k != hz)
    def _():
        await_bytes(own, tok_send)

    @pl.when(k == hz)
    def _():
        await_bytes(stats.at[pl.ds(0, 112)], stat_send)

    await_bytes(gathered.at[:, pl.ds(0, 192)], fwd_send)
    await_bytes(stats.at[pl.ds(0, 192)], statf_send)
    await_bytes(table.at[0], share_send.at[0])
    await_bytes(w1.at[pl.ds(0, 384), pl.ds(0, 512)], share_send.at[1])
    await_bytes(w1.at[pl.ds(0, 384), pl.ds(0, 512)], share_send.at[2])
    await_bytes(w2.at[0], share_send.at[3])
    local[3].wait()
    await_bytes(w2.at[0], share_recv.at[3])

    await_bytes(part_in, part_recv)
    mine = pl.ds(pl.multiple_of(32 * y, 32), 32)
    gate_up = part[mine, :].astype(F32) + jnp.sum(part_in[...].astype(F32), axis=0)
    gate, up = gate_up[:, 0:512], gate_up[:, 512:1024]
    hidden[mine, :] = (gate / (1.0 + jnp.exp(-gate)) * up).astype(BF16)
    for dy in (4, 3, 5, 2, 6, 1, 7):
        send(hidden.at[mine], hidden.at[mine], hid_send, hid_recv, place((y + dy) % NY, k, z, x))
    await_bytes(part_in, part_send)
    await_bytes(hidden.at[pl.ds(0, 224)], hid_recv)

    for kk in (0, 1):
        share = jnp.dot(hidden[...], w2[kk], preferred_element_type=F32).astype(BF16)
        for to_z in range(4):
            for to_x in range(NX):
                at = 64 * to_z + 16 * to_x
                down[to_z, to_x, kk] = share[at : at + 16, :]
    for to_z in range(4):
        for dx in (2, 1, 3):
            to = (x + dx) % NX
            send(down.at[to_z, to], down_in.at[to_z, dx - 1], dx_send, dx_recv.at[to_z], place(y, k, z, to))
    await_bytes(hidden.at[pl.ds(0, 224)], hid_send)
    for to_z in range(4):
        await_bytes(down_in.at[to_z], dx_recv.at[to_z])
        for kk in (0, 1):
            down_mid[to_z, kk] = (
                down[to_z, x, kk].astype(F32) + jnp.sum(down_in[to_z, :, kk].astype(F32), axis=0)
            ).astype(BF16)
        goal = 4 * k + to_z
        for kk in (0, 1):
            here = (goal == z) & (k == kk)

            @pl.when(here)
            def _(to_z=to_z, kk=kk):
                pltpu.make_async_copy(down_mid.at[to_z, kk], branch_in.at[z], dz_recv).start()

            @pl.when(jnp.logical_not(here))
            def _(to_z=to_z, kk=kk, goal=goal):
                send(down_mid.at[to_z, kk], branch_in.at[z], dz_send, dz_recv, place(y, kk, goal, x))

    await_bytes(down_in, dx_send)
    await_bytes(branch_in, dz_recv)
    branch = jnp.sum(branch_in[...].astype(F32), axis=0)
    own_out[...] = (own[...].astype(F32) + gate_mod * branch).astype(BF16)
    result = pltpu.make_async_copy(own_out, out, local_sem.at[5])
    result.start()
    await_bytes(branch_in.at[pl.ds(0, 7)], dz_send)

    @pl.when(k != hz)
    def _():
        await_bytes(own, dz_send)

    result.wait()


def on_device(tokens, token_frame, noise_level, modulation, gate_weight, up_weight, down_weight):
    hbm = pl.BlockSpec(memory_space=pl.ANY)
    smem = pl.BlockSpec(memory_space=pltpu.SMEM)
    vmem, dma = pltpu.VMEM, pltpu.SemaphoreType.DMA
    return pl.pallas_call(
        kernel,
        out_shape=jax.ShapeDtypeStruct((16, 384), BF16),
        in_specs=[hbm, smem, smem, hbm, hbm, hbm, hbm],
        out_specs=hbm,
        scratch_shapes=[
            vmem((16, 384), BF16),
            vmem((2, 64, 3, 384), BF16),
            vmem((768, 1024), BF16),
            vmem((2, 512, 384), BF16),
            vmem((16, 128), BF16),
            vmem((16, 16, 128), BF16),
            vmem((16, 128), BF16),
            vmem((256, 128), BF16),
            vmem((2, 256, 384), BF16),
            vmem((2, 128, 768), BF16),
            vmem((128, 256), BF16),
            vmem((256, 768), BF16),
            vmem((256, 1024), BF16),
            vmem((7, 32, 1024), BF16),
            vmem((256, 512), BF16),
            vmem((4, 4, 2, 16, 384), BF16),
            vmem((4, 3, 2, 16, 384), BF16),
            vmem((4, 2, 16, 384), BF16),
            vmem((8, 16, 384), BF16),
            vmem((16, 384), BF16),
            dma((6,)),
            dma((4,)),
            dma((4,)),
            dma,
            dma,
            dma,
            dma((4, 2)),
            dma,
            dma,
            dma,
            dma((4,)),
            dma,
            dma,
            dma,
            dma,
            dma,
            dma,
            dma,
            dma((4,)),
            dma,
            dma,
            dma,
        ],
        compiler_params=pltpu.CompilerParams(
            collective_id=0, has_side_effects=True, vmem_limit_bytes=48 << 20
        ),
        cost_estimate=pl.CostEstimate(flops=604_000_000, bytes_accessed=1_400_000, transcendentals=16384),
        name="modulated_feed_forward",
    )(tokens, token_frame, noise_level, modulation, gate_weight, up_weight, down_weight)


def solution(mesh):
    placed = (
        P("col", "row"),
        P("col"),
        P(),
        P(None, None, "row"),
        P("row", "col"),
        P("row", "col"),
        P("col", "row"),
    )
    return jax.shard_map(
        on_device, mesh=mesh, in_specs=placed, out_specs=P("col", "row"), check_vma=False
    )
```

```python
import jax
import jax.numpy as jnp
from jax import lax
from jax.experimental import pallas as pl
from jax.experimental.pallas import tpu as pltpu
from jax.sharding import PartitionSpec as P

D = 6144
EPS = 1e-06
NY, NZ, NX = 8, 8, 4
MESH = pl.DeviceIdType.MESH
F32, BF16 = jnp.float32, jnp.bfloat16


def place(y, core, z, x):
    return (y * 2 + core, z * NX + x)


def pieces(value):
    high = value.astype(BF16).astype(F32)
    rest = value - high
    middle = rest.astype(BF16).astype(F32)
    return high, middle, rest - middle


def in_lanes(lane, first, columns, base):
    for i, column in enumerate(columns):
        base = jnp.where(lane == first + i, column, base)
    return base


def send(src, dst, send_sem, recv_sem, device):
    pltpu.make_async_remote_copy(
        src, dst, send_sem, recv_sem, device_id=device, device_id_type=MESH
    ).start()


def await_bytes(ref, sem):
    pltpu.make_async_copy(ref, ref, sem).wait()


def kernel(
    tokens, frame, noise, modulation, gate_w, up_w, down_w, out,
    own, table, w1, w2, sum_out, sum_in, stat_out, stats, gathered, fields, picks,
    normed, part, part_in, hidden, down, down_in, down_mid, branch_in, levels,
    local_sem, share_send, share_recv, sum_send, sum_recv, tok_send, tok_recv,
    fwd_send, fwd_recv, stat_send, stat_recv, statf_send, statf_recv, part_send, part_recv, hid_send, hid_recv,
    dx_send, dx_recv, dz_send, dz_recv,
):
    row, col = lax.axis_index("row"), lax.axis_index("col")
    y, k, z, x = row // 2, row % 2, col // NX, col % NX
    hz = z // 4
    zz = z % 4
    sibling = place(y, 1 - k, z, x)

    own_copy = pltpu.make_async_copy(tokens, own, local_sem.at[0])
    own_copy.start()
    local = [
        pltpu.make_async_copy(modulation, table.at[k], local_sem.at[1]),
        pltpu.make_async_copy(gate_w, w1.at[pl.ds(384 * k, 384), pl.ds(0, 512)], local_sem.at[2]),
        pltpu.make_async_copy(up_w, w1.at[pl.ds(384 * k, 384), pl.ds(512, 512)], local_sem.at[3]),
        pltpu.make_async_copy(down_w, w2.at[k], local_sem.at[4]),
    ]
    for copy in local:
        copy.start()

    small = [
        pltpu.make_async_copy(frame, levels.at[0], local_sem.at[5]),
        pltpu.make_async_copy(noise, levels.at[1], local_sem.at[6]),
    ]
    for copy in small:
        copy.start()

    barrier = pltpu.get_barrier_semaphore()
    peers = [place((y + dy) % NY, (k + dk) % 2, z, x) for dy in (4, 3, 5, 2, 6, 1, 7, 0) for dk in (0, 1) if dy or dk]
    peers += [place(y, (k + dk) % 2, (z + dz) % NZ, x) for dz in (4, 3, 5, 2, 6, 1, 7) for dk in (0, 1)]
    peers += [place(y, k, z, (x + dx) % NX) for dx in (2, 1, 3)]
    for peer in peers:
        pl.semaphore_signal(barrier, inc=1, device_id=peer, device_id_type=MESH)

    own_copy.wait()
    wide = own[...].astype(F32)
    lane = lax.broadcasted_iota(jnp.int32, (16, 128), 1)
    sublane = lax.broadcasted_iota(jnp.int32, (16, 128), 0)
    zero = jnp.zeros((16, 128), F32)
    columns = pieces(jnp.sum(wide, axis=1, keepdims=True)) + pieces(jnp.sum(wide * wide, axis=1, keepdims=True))
    sums = in_lanes(lane, 0, columns, zero).astype(BF16)
    sum_out[...] = sums
    sum_in[row] = sums
    for copy in small:
        copy.wait()
    onehot = zero
    for t in range(16):
        level = levels[1, levels[0, t]]
        onehot = jnp.where((sublane == t) & (lane == level), 1.0, onehot)

    pl.semaphore_wait(barrier, len(peers))

    for dy in (4, 3, 5, 2, 6, 1, 7, 0):
        for dk in (0, 1):
            if dy or dk:
                send(sum_out, sum_in.at[row], sum_send, sum_recv, place((y + dy) % NY, (k + dk) % 2, z, x))
    block = pl.ds(64 * zz + 16 * x, 16)
    for dz in (4, 3, 5, 2, 6, 1, 7):
        send(own, gathered.at[k, block], tok_send, tok_recv.at[zz, k], place(y, hz, (z + dz) % NZ, x))

    @pl.when(k == hz)
    def _():
        pltpu.make_async_copy(own, gathered.at[k, block], tok_recv.at[zz, k]).start()

    @pl.when(k != hz)
    def _():
        send(own, gathered.at[k, block], tok_send, tok_recv.at[zz, k], sibling)

    send(modulation, table.at[k], share_send.at[0], share_recv.at[0], sibling)
    send(gate_w, w1.at[pl.ds(384 * k, 384), pl.ds(0, 512)], share_send.at[1], share_recv.at[1], sibling)
    send(up_w, w1.at[pl.ds(384 * k, 384), pl.ds(512, 512)], share_send.at[2], share_recv.at[2], sibling)
    send(down_w, w2.at[k], share_send.at[3], share_recv.at[3], sibling)

    await_bytes(sum_in.at[pl.ds(0, 15)], sum_recv)
    total = jnp.sum(sum_in[...].astype(F32), axis=0)
    center = jnp.sum(jnp.where(lane < 3, total, 0.0), axis=1, keepdims=True) / D
    square = jnp.sum(jnp.where((lane >= 3) & (lane < 6), total, 0.0), axis=1, keepdims=True) / D
    scale = lax.rsqrt(square - center * center + EPS)
    stat_out[...] = in_lanes(lane, 64, pieces(center) + pieces(scale), onehot).astype(BF16)

    @pl.when(k == hz)
    def _():
        for dz in (4, 3, 5, 2, 6, 1, 7):
            send(stat_out, stats.at[block], stat_send, stat_recv.at[zz], place(y, k, (z + dz) % NZ, x))
        pltpu.make_async_copy(stat_out, stats.at[block], stat_recv.at[zz]).start()

    for i in range(4):
        from_z = (zz + i) % 4
        came = pl.ds(64 * from_z + 16 * x, 16)
        for kk in (0, 1):
            await_bytes(gathered.at[kk, came], tok_recv.at[from_z, kk])
            for dx in (2, 1, 3):
                send(gathered.at[kk, came], gathered.at[kk, came], fwd_send, fwd_recv, place(y, k, z, (x + dx) % NX))

    local[0].wait()
    await_bytes(table.at[0], share_recv.at[0])
    for kk in (0, 1):
        fields[kk, 64:128, :] = jnp.zeros((64, 768), BF16)
        fields[kk, 0:64, 0:384] = table[kk, 0]
        fields[kk, 0:64, 384:768] = table[kk, 1]
    gate_mod = jnp.dot(onehot.astype(BF16)[:, 0:64], table[k, 2], preferred_element_type=F32)
    source = lax.broadcasted_iota(jnp.int32, (128, 256), 0)
    target = lax.broadcasted_iota(jnp.int32, (128, 256), 1)
    picks[...] = jnp.where(
        ((target < 128) & (source >= 64) & (source < 67)) | ((target >= 128) & (source >= 67) & (source < 70)), 1.0, 0.0
    ).astype(BF16)

    for i in range(4):
        from_z = (zz + i) % 4
        came = pl.ds(64 * from_z + 16 * x, 16)
        await_bytes(stats.at[came], stat_recv.at[from_z])
        for dx in (2, 1, 3):
            send(stats.at[came], stats.at[came], statf_send, statf_recv, place(y, k, z, (x + dx) % NX))
    await_bytes(gathered.at[:, pl.ds(0, 192)], fwd_recv)
    await_bytes(stats.at[pl.ds(0, 192)], statf_recv)

    table_of = stats[...]
    moments = jnp.dot(table_of, picks[...], preferred_element_type=F32)
    for kk in (0, 1):
        mods = jnp.dot(table_of, fields[kk], preferred_element_type=F32)
        for part_of in range(3):
            at = slice(128 * part_of, 128 * part_of + 128)
            after = slice(384 + 128 * part_of, 512 + 128 * part_of)
            normed[:, 384 * kk + 128 * part_of : 384 * kk + 128 * part_of + 128] = (
                (gathered[kk, :, at].astype(F32) - moments[:, 0:128]) * moments[:, 128:256] * (1.0 + mods[:, after])
                + mods[:, at]
            ).astype(BF16)

    local[1].wait()
    local[2].wait()
    await_bytes(w1.at[pl.ds(0, 384), pl.ds(0, 512)], share_recv.at[1])
    await_bytes(w1.at[pl.ds(0, 384), pl.ds(0, 512)], share_recv.at[2])
    for n in range(2):
        at = slice(512 * n, 512 * n + 512)
        part[:, at] = jnp.dot(normed[...], w1[:, at], preferred_element_type=F32).astype(BF16)
    for dy in (4, 3, 5, 2, 6, 1, 7):
        to = (y + dy) % NY
        send(part.at[pl.ds(32 * to, 32)], part_in.at[dy - 1], part_send, part_recv, place(to, k, z, x))

    await_bytes(sum_in.at[pl.ds(0, 15)], sum_send)
    await_bytes(gathered.at[0, pl.ds(0, 112)], tok_send)

    @pl.when(k != hz)
    def _():
        await_bytes(own, tok_send)

    @pl.when(k == hz)
    def _():
        await_bytes(stats.at[pl.ds(0, 112)], stat_send)

    await_bytes(gathered.at[:, pl.ds(0, 192)], fwd_send)
    await_bytes(stats.at[pl.ds(0, 192)], statf_send)
    await_bytes(table.at[0], share_send.at[0])
    await_bytes(w1.at[pl.ds(0, 384), pl.ds(0, 512)], share_send.at[1])
    await_bytes(w1.at[pl.ds(0, 384), pl.ds(0, 512)], share_send.at[2])
    await_bytes(w2.at[0], share_send.at[3])
    local[3].wait()
    await_bytes(w2.at[0], share_recv.at[3])

    await_bytes(part_in, part_recv)
    mine = pl.ds(pl.multiple_of(32 * y, 32), 32)
    gate_up = part[mine, :].astype(F32) + jnp.sum(part_in[...].astype(F32), axis=0)
    gate, up = gate_up[:, 0:512], gate_up[:, 512:1024]
    hidden[mine, :] = (gate / (1.0 + jnp.exp(-gate)) * up).astype(BF16)
    for dy in (4, 3, 5, 2, 6, 1, 7):
        send(hidden.at[mine], hidden.at[mine], hid_send, hid_recv, place((y + dy) % NY, k, z, x))
    await_bytes(part_in, part_send)
    await_bytes(hidden.at[pl.ds(0, 224)], hid_recv)

    for kk in (0, 1):
        share = jnp.dot(hidden[...], w2[kk], preferred_element_type=F32).astype(BF16)
        for to_z in range(4):
            for to_x in range(NX):
                at = 64 * to_z + 16 * to_x
                down[to_z, to_x, kk] = share[at : at + 16, :]
    for to_z in range(4):
        for dx in (2, 1, 3):
            to = (x + dx) % NX
            send(down.at[to_z, to], down_in.at[to_z, dx - 1], dx_send, dx_recv.at[to_z], place(y, k, z, to))
    await_bytes(hidden.at[pl.ds(0, 224)], hid_send)
    for to_z in range(4):
        await_bytes(down_in.at[to_z], dx_recv.at[to_z])
        for kk in (0, 1):
            down_mid[to_z, kk] = (
                down[to_z, x, kk].astype(F32) + jnp.sum(down_in[to_z, :, kk].astype(F32), axis=0)
            ).astype(BF16)
        goal = 4 * k + to_z
        for kk in (0, 1):
            here = (goal == z) & (k == kk)

            @pl.when(here)
            def _(to_z=to_z, kk=kk):
                pltpu.make_async_copy(down_mid.at[to_z, kk], branch_in.at[z], dz_recv).start()

            @pl.when(jnp.logical_not(here))
            def _(to_z=to_z, kk=kk, goal=goal):
                send(down_mid.at[to_z, kk], branch_in.at[z], dz_send, dz_recv, place(y, kk, goal, x))

    await_bytes(down_in, dx_send)
    await_bytes(branch_in, dz_recv)
    branch = jnp.sum(branch_in[...].astype(F32), axis=0)
    out[...] = (own[...].astype(F32) + gate_mod * branch).astype(BF16)
    await_bytes(branch_in.at[pl.ds(0, 7)], dz_send)

    @pl.when(k != hz)
    def _():
        await_bytes(own, dz_send)


def on_device(tokens, token_frame, noise_level, modulation, gate_weight, up_weight, down_weight):
    hbm = pl.BlockSpec(memory_space=pltpu.HBM)
    vmem, dma = pltpu.VMEM, pltpu.SemaphoreType.DMA
    return pl.pallas_call(
        kernel,
        out_shape=jax.ShapeDtypeStruct((16, 384), BF16),
        in_specs=[hbm, hbm, hbm, hbm, hbm, hbm, hbm],
        out_specs=pl.BlockSpec(memory_space=pltpu.VMEM),
        scratch_shapes=[
            vmem((16, 384), BF16),
            vmem((2, 3, 64, 384), BF16),
            vmem((768, 1024), BF16),
            vmem((2, 512, 384), BF16),
            vmem((16, 128), BF16),
            vmem((16, 16, 128), BF16),
            vmem((16, 128), BF16),
            vmem((256, 128), BF16),
            vmem((2, 256, 384), BF16),
            vmem((2, 128, 768), BF16),
            vmem((128, 256), BF16),
            vmem((256, 768), BF16),
            vmem((256, 1024), BF16),
            vmem((7, 32, 1024), BF16),
            vmem((256, 512), BF16),
            vmem((4, 4, 2, 16, 384), BF16),
            vmem((4, 3, 2, 16, 384), BF16),
            vmem((4, 2, 16, 384), BF16),
            vmem((8, 16, 384), BF16),
            pltpu.SMEM((2, 16), jnp.int32),
            dma((7,)),
            dma((4,)),
            dma((4,)),
            dma,
            dma,
            dma,
            dma((4, 2)),
            dma,
            dma,
            dma,
            dma((4,)),
            dma,
            dma,
            dma,
            dma,
            dma,
            dma,
            dma,
            dma((4,)),
            dma,
            dma,
        ],
        compiler_params=pltpu.CompilerParams(
            collective_id=0, has_side_effects=True, vmem_limit_bytes=60 << 20
        ),
        cost_estimate=pl.CostEstimate(flops=604_000_000, bytes_accessed=1_400_000, transcendentals=16384),
        name="modulated_feed_forward",
    )(tokens, token_frame, noise_level, jnp.transpose(modulation, (1, 0, 2)), gate_weight, up_weight, down_weight)


def solution(mesh):
    placed = (
        P("col", "row"),
        P("col"),
        P(),
        P(None, None, "row"),
        P("row", "col"),
        P("row", "col"),
        P("col", "row"),
    )
    return jax.shard_map(
        on_device, mesh=mesh, in_specs=placed, out_specs=P("col", "row"), check_vma=False
    )
```

```python
import jax
import jax.numpy as jnp
from jax import lax
from jax.experimental import pallas as pl
from jax.experimental.pallas import tpu as pltpu
from jax.sharding import PartitionSpec as P

D = 6144
EPS = 1e-06
NY, NZ, NX = 8, 8, 4
MESH = pl.DeviceIdType.MESH
F32, BF16 = jnp.float32, jnp.bfloat16


def place(y, core, z, x):
    return (y * 2 + core, z * NX + x)


def pieces(value):
    high = value.astype(BF16).astype(F32)
    rest = value - high
    middle = rest.astype(BF16).astype(F32)
    return high, middle, rest - middle


def in_lanes(lane, first, columns, base):
    for i, column in enumerate(columns):
        base = jnp.where(lane == first + i, column, base)
    return base


def send(src, dst, send_sem, recv_sem, device):
    pltpu.make_async_remote_copy(
        src, dst, send_sem, recv_sem, device_id=device, device_id_type=MESH
    ).start()


def await_bytes(ref, sem):
    pltpu.make_async_copy(ref, ref, sem).wait()


class Waits:
    def __init__(self):
        self.owed = {}

    def owe(self, name, ref, sem, when=None):
        self.owed.setdefault(name, []).append((ref, sem, when))

    def take(self, *names):
        for name in names:
            for ref, sem, when in self.owed.pop(name):
                if when is None:
                    await_bytes(ref, sem)
                else:
                    pl.when(when)(lambda ref=ref, sem=sem: await_bytes(ref, sem))


def kernel(
    tokens, frame, noise, modulation, gate_w, up_w, down_w, out,
    own, table, w1, w2, sum_out, sum_in, stat_out, stats, gathered, fields, picks,
    normed, part, part_in, relay, hidden, down, down_in, down_relay, down_mid, branch_in, levels,
    local_sem, share_send, share_recv, sum_send, sum_recv, tok_send, tok_recv,
    fwd_send, fwd_recv, stat_send, stat_recv, statf_send, statf_recv, part_send, part_recv, hid_send, hid_recv,
    dx_send, dx_recv, dz_send, dz_recv,
):
    row, col = lax.axis_index("row"), lax.axis_index("col")
    y, k, z, x = row // 2, row % 2, col // NX, col % NX
    hz = z // 4
    zz = z % 4
    way = 1 - 2 * k
    sibling = place(y, 1 - k, z, x)
    waits = Waits()

    def at_y(step):
        return lax.rem(y + 8 + step * way, NY)

    def at_x(step):
        return lax.rem(x + 4 + step * way, NX)

    def to_y(target):
        return place(target, k, z, x)

    def to_x(target):
        return place(y, k, z, target)

    own_copy = pltpu.make_async_copy(tokens, own, local_sem.at[0])
    own_copy.start()
    small = [
        pltpu.make_async_copy(frame, levels.at[0], local_sem.at[5]),
        pltpu.make_async_copy(noise, levels.at[1], local_sem.at[6]),
    ]
    for copy in small:
        copy.start()
    barrier = pltpu.get_barrier_semaphore()
    peers = [place((y + dy) % NY, (k + dk) % 2, z, x) for dy in (4, 3, 5, 2, 6, 1, 7, 0) for dk in (0, 1) if dy or dk]
    peers += [place(y, (k + dk) % 2, (z + dz) % NZ, x) for dz in (4, 3, 5, 2, 6, 1, 7) for dk in (0, 1)]
    peers += [place(y, k, z, (x + dx) % NX) for dx in (2, 1, 3)]
    for peer in peers:
        pl.semaphore_signal(barrier, inc=1, device_id=peer, device_id_type=MESH)

    own_copy.wait()
    wide = own[...].astype(F32)
    lane = lax.broadcasted_iota(jnp.int32, (16, 128), 1)
    sublane = lax.broadcasted_iota(jnp.int32, (16, 128), 0)
    zero = jnp.zeros((16, 128), F32)
    square = jnp.sum(wide * wide, axis=1, keepdims=True)
    spread_out = jnp.where(lane == sublane, jnp.sum(wide, axis=1, keepdims=True), zero)
    spread_out = jnp.where(lane == sublane + 16, square, spread_out)
    sums = jnp.sum(spread_out, axis=0, keepdims=True)
    sum_out[0] = sums
    sum_in[row] = sums

    pl.semaphore_wait(barrier, len(peers))

    for dy in (4, 3, 5, 2, 6, 1, 7, 0):
        for dk in (0, 1):
            if dy or dk:
                send(sum_out.at[0], sum_in.at[row], sum_send, sum_recv, place((y + dy) % NY, (k + dk) % 2, z, x))
    waits.owe("sum_send", sum_in.at[pl.ds(0, 15)], sum_send)
    waits.owe("sum_recv", sum_in.at[pl.ds(0, 15)], sum_recv)
    block = pl.ds(64 * zz + 16 * x, 16)
    for dz in (4, 3, 5, 2, 6, 1, 7):
        send(own, gathered.at[k, block], tok_send, tok_recv.at[zz, k], place(y, hz, (z + dz) % NZ, x))

    @pl.when(k == hz)
    def _():
        pltpu.make_async_copy(own, gathered.at[k, block], tok_recv.at[zz, k]).start()

    @pl.when(k != hz)
    def _():
        send(own, gathered.at[k, block], tok_send, tok_recv.at[zz, k], sibling)

    waits.owe("tok_send", gathered.at[0, pl.ds(0, 112)], tok_send)
    waits.owe("tok_send", own, tok_send, k != hz)

    half = w1.at[pl.ds(0, 384), pl.ds(0, 512)]
    rows = pl.ds(384 * k, 384)
    for i, (source, goal, like) in enumerate(
        (
            (modulation, table.at[k], table.at[0]),
            (gate_w, w1.at[rows, pl.ds(0, 512)], half),
            (up_w, w1.at[rows, pl.ds(512, 512)], half),
            (down_w, w2.at[k], w2.at[0]),
        )
    ):
        pltpu.make_async_copy(source, goal, local_sem.at[1 + i]).start()
        send(source, goal, share_send.at[i], share_recv.at[i], sibling)
        waits.owe("share_send", like, share_send.at[i])
        waits.owe(("share_recv", i), like, share_recv.at[i])
        waits.owe(("share_recv", i), like, local_sem.at[1 + i])

    for copy in small:
        copy.wait()
    onehot = zero
    for t in range(16):
        level = levels[1, levels[0, t]]
        onehot = jnp.where((sublane == t) & (lane == level), 1.0, onehot)

    waits.take("sum_recv")
    total = jnp.broadcast_to(jnp.sum(sum_in[:, 0, :], axis=0, keepdims=True), (16, 128))
    center = jnp.sum(jnp.where(lane == sublane, total, zero), axis=1, keepdims=True) / D
    square = jnp.sum(jnp.where(lane == sublane + 16, total, zero), axis=1, keepdims=True) / D
    scale = lax.rsqrt(square - center * center + EPS)
    stat_out[...] = in_lanes(lane, 64, pieces(center) + pieces(scale), onehot).astype(BF16)

    @pl.when(k == hz)
    def _():
        for dz in (4, 3, 5, 2, 6, 1, 7):
            send(stat_out, stats.at[block], stat_send, stat_recv.at[zz], place(y, k, (z + dz) % NZ, x))
        pltpu.make_async_copy(stat_out, stats.at[block], stat_recv.at[zz]).start()

    waits.owe("stat_send", stats.at[pl.ds(0, 112)], stat_send, k == hz)

    for i in range(4):
        from_z = (zz + i) % 4
        came = pl.ds(64 * from_z + 16 * x, 16)
        for kk in (0, 1):
            await_bytes(gathered.at[kk, came], tok_recv.at[from_z, kk])
            for dx in (2, 1, 3):
                send(gathered.at[kk, came], gathered.at[kk, came], fwd_send, fwd_recv, to_x((x + dx) % NX))
    waits.owe("fwd_send", gathered.at[:, pl.ds(0, 192)], fwd_send)
    waits.owe("fwd_recv", gathered.at[:, pl.ds(0, 192)], fwd_recv)

    waits.take(("share_recv", 0))
    for kk in (0, 1):
        fields[kk, 64:128, :] = jnp.zeros((64, 768), BF16)
        fields[kk, 0:64, 0:384] = table[kk, 0]
        fields[kk, 0:64, 384:768] = table[kk, 1]
    gate_mod = jnp.dot(onehot.astype(BF16)[:, 0:64], table[k, 2], preferred_element_type=F32)
    source = lax.broadcasted_iota(jnp.int32, (128, 256), 0)
    target = lax.broadcasted_iota(jnp.int32, (128, 256), 1)
    picks[...] = jnp.where(
        ((target < 128) & (source >= 64) & (source < 67)) | ((target >= 128) & (source >= 67) & (source < 70)), 1.0, 0.0
    ).astype(BF16)

    for i in range(4):
        from_z = (zz + i) % 4
        came = pl.ds(64 * from_z + 16 * x, 16)
        await_bytes(stats.at[came], stat_recv.at[from_z])
        for dx in (2, 1, 3):
            send(stats.at[came], stats.at[came], statf_send, statf_recv, to_x((x + dx) % NX))
    waits.owe("statf_send", stats.at[pl.ds(0, 192)], statf_send)
    waits.owe("statf_recv", stats.at[pl.ds(0, 192)], statf_recv)
    waits.take("fwd_recv")
    waits.take("statf_recv")

    table_of = stats[...]
    moments = jnp.dot(table_of, picks[...], preferred_element_type=F32)
    for kk in (0, 1):
        mods = jnp.dot(table_of, fields[kk], preferred_element_type=F32)
        for part_of in range(3):
            at = slice(128 * part_of, 128 * part_of + 128)
            after = slice(384 + 128 * part_of, 512 + 128 * part_of)
            normed[:, 384 * kk + 128 * part_of : 384 * kk + 128 * part_of + 128] = (
                (gathered[kk, :, at].astype(F32) - moments[:, 0:128]) * moments[:, 128:256] * (1.0 + mods[:, after])
                + mods[:, at]
            ).astype(BF16)

    waits.take(("share_recv", 1), ("share_recv", 2))
    for n in range(2):
        at = slice(512 * n, 512 * n + 512)
        part[:, at] = jnp.dot(normed[...], w1[:, at], preferred_element_type=F32).astype(BF16)

    def of_y(target):
        return pl.ds(pl.multiple_of(32 * target, 32), 32)

    for slot, (goal, via) in enumerate(((-4, -2), (-3, -1), (3, 1), (-1, -1), (1, 1))):
        send(part.at[of_y(at_y(goal))], part_in.at[slot], part_send, part_recv.at[slot], to_y(at_y(via)))
        waits.owe(("part", slot), part_in.at[slot], part_recv.at[slot])
    waits.owe("part_send", part_in, part_send)
    waits.take(("part", 2))
    relay[1] = (part[of_y(at_y(2)), :].astype(F32) + part_in[2].astype(F32)).astype(BF16)
    send(relay.at[1], part_in.at[6], part_send, part_recv.at[6], to_y(at_y(2)))
    waits.take(("part", 1), ("part", 0))
    relay[0] = (part[of_y(at_y(-2)), :].astype(F32) + part_in[1].astype(F32) + part_in[0].astype(F32)).astype(BF16)
    send(relay.at[0], part_in.at[5], part_send, part_recv.at[5], to_y(at_y(-2)))
    waits.owe(("part", 5), part_in.at[5], part_recv.at[5])
    waits.owe(("part", 6), part_in.at[6], part_recv.at[6])
    waits.take("sum_send", "tok_send", "fwd_send", "stat_send", "statf_send", "share_send")
    waits.take(("share_recv", 3))
    waits.take(("part", 3), ("part", 4), ("part", 6), ("part", 5))

    mine = of_y(y)
    gate_up = part[mine, :].astype(F32) + jnp.sum(part_in[3:7].astype(F32), axis=0)
    gate, up = gate_up[:, 0:512], gate_up[:, 512:1024]
    hidden[mine, :] = (gate / (1.0 + jnp.exp(-gate)) * up).astype(BF16)
    for slot, step in enumerate((2, -2, 1, -1)):
        send(hidden.at[mine], hidden.at[mine], hid_send, hid_recv.at[min(slot, 2)], to_y(at_y(step)))
    waits.owe("hid_a", hidden.at[pl.ds(0, 32)], hid_recv.at[0])
    waits.owe("hid_b", hidden.at[pl.ds(0, 32)], hid_recv.at[1])
    waits.take("part_send")
    waits.take("hid_a")
    came = of_y(at_y(-2))
    send(hidden.at[came], hidden.at[came], hid_send, hid_recv.at[2], to_y(at_y(2)))
    send(hidden.at[came], hidden.at[came], hid_send, hid_recv.at[2], to_y(at_y(1)))
    waits.take("hid_b")
    came = of_y(at_y(2))
    send(hidden.at[came], hidden.at[came], hid_send, hid_recv.at[2], to_y(at_y(-1)))
    waits.owe("hid_send", hidden.at[pl.ds(0, 224)], hid_send)
    waits.owe("hid_rest", hidden.at[pl.ds(0, 160)], hid_recv.at[2])
    waits.take("hid_rest")

    for kk in (0, 1):
        share = jnp.dot(hidden[...], w2[kk], preferred_element_type=F32).astype(BF16)
        for to_z in range(4):
            for goal_x in range(NX):
                at = 64 * to_z + 16 * goal_x
                down[to_z, goal_x, kk] = share[at : at + 16, :]
    for to_z in range(4):
        send(down.at[to_z, at_x(2)], down_in.at[to_z, 0], dx_send, dx_recv.at[to_z, 0], to_x(at_x(-1)))
    for to_z in range(4):
        send(down.at[to_z, at_x(1)], down_in.at[to_z, 1], dx_send, dx_recv.at[to_z, 1], to_x(at_x(1)))
    waits.take("hid_send")
    for to_z in range(4):
        await_bytes(down_in.at[to_z, 0], dx_recv.at[to_z, 0])
        down_relay[to_z] = (down[to_z, at_x(-1)].astype(F32) + down_in[to_z, 0].astype(F32)).astype(BF16)
        send(down_relay.at[to_z], down_in.at[to_z, 2], dx_send, dx_recv.at[to_z, 2], to_x(at_x(-1)))
    for to_z in range(4):
        await_bytes(down_in.at[to_z, 1], dx_recv.at[to_z, 1])
        await_bytes(down_in.at[to_z, 2], dx_recv.at[to_z, 2])
        down_mid[to_z] = (
            down[to_z, x].astype(F32) + down_in[to_z, 1].astype(F32) + down_in[to_z, 2].astype(F32)
        ).astype(BF16)
        goal = 4 * k + to_z
        for kk in (0, 1):
            here = (goal == z) & (k == kk)

            @pl.when(here)
            def _(to_z=to_z, kk=kk):
                pltpu.make_async_copy(down_mid.at[to_z, kk], branch_in.at[z], dz_recv).start()

            @pl.when(jnp.logical_not(here))
            def _(to_z=to_z, kk=kk, goal=goal):
                send(down_mid.at[to_z, kk], branch_in.at[z], dz_send, dz_recv, place(y, kk, goal, x))

    waits.owe("dx_send", down_in, dx_send)
    waits.owe("dz_recv", branch_in, dz_recv)
    waits.owe("dz_send", branch_in.at[pl.ds(0, 7)], dz_send)
    waits.owe("dz_send", own, dz_send, k != hz)
    waits.take("dz_recv")
    branch = jnp.sum(branch_in[...].astype(F32), axis=0)
    out[...] = (own[...].astype(F32) + gate_mod * branch).astype(BF16)
    waits.take("dx_send", "dz_send")


def on_device(tokens, token_frame, noise_level, modulation, gate_weight, up_weight, down_weight):
    hbm = pl.BlockSpec(memory_space=pltpu.HBM)
    vmem, dma = pltpu.VMEM, pltpu.SemaphoreType.DMA
    return pl.pallas_call(
        kernel,
        out_shape=jax.ShapeDtypeStruct((16, 384), BF16),
        in_specs=[hbm, hbm, hbm, hbm, hbm, hbm, hbm],
        out_specs=pl.BlockSpec(memory_space=pltpu.VMEM),
        scratch_shapes=[
            vmem((16, 384), BF16),
            vmem((2, 3, 64, 384), BF16),
            vmem((768, 1024), BF16),
            vmem((2, 512, 384), BF16),
            vmem((1, 1, 128), F32),
            vmem((16, 1, 128), F32),
            vmem((16, 128), BF16),
            vmem((256, 128), BF16),
            vmem((2, 256, 384), BF16),
            vmem((2, 128, 768), BF16),
            vmem((128, 256), BF16),
            vmem((256, 768), BF16),
            vmem((256, 1024), BF16),
            vmem((7, 32, 1024), BF16),
            vmem((2, 32, 1024), BF16),
            vmem((256, 512), BF16),
            vmem((4, 4, 2, 16, 384), BF16),
            vmem((4, 3, 2, 16, 384), BF16),
            vmem((4, 2, 16, 384), BF16),
            vmem((4, 2, 16, 384), BF16),
            vmem((8, 16, 384), BF16),
            pltpu.SMEM((2, 16), jnp.int32),
            dma((7,)),
            dma((4,)),
            dma((4,)),
            dma,
            dma,
            dma,
            dma((4, 2)),
            dma,
            dma,
            dma,
            dma((4,)),
            dma,
            dma,
            dma,
            dma((7,)),
            dma,
            dma((3,)),
            dma,
            dma((4, 3)),
            dma,
            dma,
        ],
        compiler_params=pltpu.CompilerParams(
            collective_id=0, has_side_effects=True, vmem_limit_bytes=60 << 20
        ),
        cost_estimate=pl.CostEstimate(flops=604_000_000, bytes_accessed=1_400_000, transcendentals=16384),
        name="modulated_feed_forward",
    )(tokens, token_frame, noise_level, jnp.transpose(modulation, (1, 0, 2)), gate_weight, up_weight, down_weight)


def solution(mesh):
    placed = (
        P("col", "row"),
        P("col"),
        P(),
        P(None, None, "row"),
        P("row", "col"),
        P("row", "col"),
        P("col", "row"),
    )
    return jax.shard_map(
        on_device, mesh=mesh, in_specs=placed, out_specs=P("col", "row"), check_vma=False
    )
```

```python
import jax
import jax.numpy as jnp
from jax import lax
from jax.experimental import pallas as pl
from jax.experimental.pallas import tpu as pltpu
from jax.sharding import PartitionSpec as P

D = 6144
EPS = 1e-06
NY, NZ, NX = 8, 8, 4
MESH = pl.DeviceIdType.MESH
F32, BF16 = jnp.float32, jnp.bfloat16


def place(y, core, z, x):
    return (y * 2 + core, z * NX + x)


def pieces(value):
    high = value.astype(BF16).astype(F32)
    rest = value - high
    middle = rest.astype(BF16).astype(F32)
    return high, middle, rest - middle


def in_lanes(lane, first, columns, base):
    for i, column in enumerate(columns):
        base = jnp.where(lane == first + i, column, base)
    return base


def send(src, dst, send_sem, recv_sem, device):
    pltpu.make_async_remote_copy(
        src, dst, send_sem, recv_sem, device_id=device, device_id_type=MESH
    ).start()


def await_bytes(ref, sem):
    pltpu.make_async_copy(ref, ref, sem).wait()


class Waits:
    def __init__(self):
        self.owed = {}

    def owe(self, name, ref, sem, when=None):
        self.owed.setdefault(name, []).append((ref, sem, when))

    def take(self, *names):
        for name in names:
            for ref, sem, when in self.owed.pop(name):
                if when is None:
                    await_bytes(ref, sem)
                else:
                    pl.when(when)(lambda ref=ref, sem=sem: await_bytes(ref, sem))


def kernel(
    tokens, frame, noise, modulation, gate_w, up_w, down_w, out,
    own, table, w1, w2, sum_out, sum_in, stat_out, stats, gathered, fields, picks,
    normed, part, part_in, relay, hidden, down, down_in, down_relay, down_mid, branch_in, levels,
    local_sem, share_send, share_recv, sum_send, sum_recv, tok_send, tok_recv,
    fwd_send, fwd_recv, stat_send, stat_recv, part_send, part_recv, hid_send, hid_recv,
    dx_send, dx_recv, dz_send, dz_recv,
):
    row, col = lax.axis_index("row"), lax.axis_index("col")
    y, k, z, x = row // 2, row % 2, col // NX, col % NX
    hz = z // 4
    zz = z % 4
    way = 1 - 2 * k
    sibling = place(y, 1 - k, z, x)
    waits = Waits()

    def at_y(step):
        return lax.rem(y + 8 + step * way, NY)

    def at_x(step):
        return lax.rem(x + 4 + step * way, NX)

    def to_y(target):
        return place(target, k, z, x)

    def to_x(target):
        return place(y, k, z, target)

    upper = zz // 2
    outward = [zz, 1 - zz + 4 * upper, 2 - upper, 3 - 3 * upper]
    holds = 1 - (k - hz) * (k - hz)
    near_first = [outward[i] * holds + outward[3 - i] * (1 - holds) for i in range(4)]
    around_z = {dz: lax.rem(z + dz, NZ) for dz in range(1, NZ)}
    around_y = {dy: lax.rem(y + dy, NY) for dy in range(NY)}
    around_x = {dx: lax.rem(x + dx, NX) for dx in range(1, NX)}
    far_z, far_y = (4, 3, 5, 2, 6, 1, 7), (4, 3, 5, 2, 6, 1, 7, 0)

    own_copy = pltpu.make_async_copy(tokens, own, local_sem.at[0])
    own_copy.start()
    small = [
        pltpu.make_async_copy(frame, levels.at[0], local_sem.at[5]),
        pltpu.make_async_copy(noise, levels.at[1], local_sem.at[6]),
    ]
    for copy in small:
        copy.start()
    barrier = pltpu.get_barrier_semaphore()
    peers = [place(y, core, around_z[dz], x) for dz in far_z for core in (k, 1 - k)]
    peers += [place(around_y[dy], core, z, x) for dy in far_y for core in (k, 1 - k)][:-2] + [sibling]
    peers += [to_x(around_x[dx]) for dx in (2, 1, 3)]
    for peer in peers:
        pl.semaphore_signal(barrier, inc=1, device_id=peer, device_id_type=MESH)
    for i in range(4):
        from_z = 4 * k + i

        @pl.when(from_z != z)
        def _(from_z=from_z):
            for dx in (2, 1, 3):
                pl.semaphore_signal(barrier, inc=1, device_id=place(y, k, from_z, around_x[dx]), device_id_type=MESH)

    own_copy.wait()
    wide = own[...].astype(F32)
    lane = lax.broadcasted_iota(jnp.int32, (16, 128), 1)
    sublane = lax.broadcasted_iota(jnp.int32, (16, 128), 0)
    zero = jnp.zeros((16, 128), F32)
    square = jnp.sum(wide * wide, axis=1, keepdims=True)
    spread_out = jnp.where(lane == sublane, jnp.sum(wide, axis=1, keepdims=True), zero)
    spread_out = jnp.where(lane == sublane + 16, square, spread_out)
    sums = jnp.sum(spread_out, axis=0, keepdims=True)
    sum_out[0] = sums
    sum_in[row] = sums

    pl.semaphore_wait(barrier, len(peers) + 21 * holds)

    block = pl.ds(64 * zz + 16 * x, 16)
    for dz in (4, 3, 5, 2, 6, 1, 7):
        send(own, gathered.at[k, block], tok_send, tok_recv.at[zz, k], place(y, hz, around_z[dz], x))

    @pl.when(k == hz)
    def _():
        pltpu.make_async_copy(own, gathered.at[k, block], tok_recv.at[zz, k]).start()

    @pl.when(k != hz)
    def _():
        send(own, gathered.at[k, block], tok_send, tok_recv.at[zz, k], sibling)

    waits.owe("tok_send", gathered.at[0, pl.ds(0, 112)], tok_send)
    waits.owe("tok_send", own, tok_send, k != hz)

    for dy in far_y:
        for core in (k, 1 - k) if dy else (1 - k,):
            send(sum_out.at[0], sum_in.at[row], sum_send, sum_recv, place(around_y[dy], core, z, x))
    waits.owe("sum_send", sum_in.at[pl.ds(0, 15)], sum_send)
    waits.owe("sum_recv", sum_in.at[pl.ds(0, 15)], sum_recv)

    half = w1.at[pl.ds(0, 384), pl.ds(0, 512)]
    rows = pl.ds(384 * k, 384)
    for i, (source, goal, like) in enumerate(
        (
            (modulation, table.at[k], table.at[0]),
            (gate_w, w1.at[rows, pl.ds(0, 512)], half),
            (up_w, w1.at[rows, pl.ds(512, 512)], half),
            (down_w, w2.at[k], w2.at[0]),
        )
    ):
        pltpu.make_async_copy(source, goal, local_sem.at[1 + i]).start()
        send(source, goal, share_send.at[i], share_recv.at[i], sibling)
        waits.owe("share_send", like, share_send.at[i])
        waits.owe(("share_recv", i), like, share_recv.at[i])
        waits.owe(("share_recv", i), like, local_sem.at[1 + i])

    for copy in small:
        copy.wait()
    onehot = zero
    for t in range(16):
        level = levels[1, levels[0, t]]
        onehot = jnp.where((sublane == t) & (lane == level), 1.0, onehot)

    waits.take("sum_recv")
    total = jnp.broadcast_to(jnp.sum(sum_in[:, 0, :], axis=0, keepdims=True), (16, 128))
    center = jnp.sum(jnp.where(lane == sublane, total, zero), axis=1, keepdims=True) / D
    square = jnp.sum(jnp.where(lane == sublane + 16, total, zero), axis=1, keepdims=True) / D
    scale = lax.rsqrt(square - center * center + EPS)
    stat_out[...] = in_lanes(lane, 64, pieces(center) + pieces(scale), onehot).astype(BF16)

    @pl.when(k == hz)
    def _():
        for dz in far_z:
            for to in (around_x[2], around_x[1], around_x[3], x):
                send(stat_out, stats.at[block], stat_send, stat_recv, place(y, k, around_z[dz], to))
        for dx in (2, 1, 3):
            send(stat_out, stats.at[block], stat_send, stat_recv, to_x(around_x[dx]))
        pltpu.make_async_copy(stat_out, stats.at[block], stat_recv).start()

    waits.owe("stat_send", stats.at[pl.ds(0, 240)], stat_send, k == hz)
    waits.owe("stat_send", stats, stat_send, k == hz)
    waits.owe("stat_recv", stats, stat_recv)

    for from_z in near_first:
        came = pl.ds(64 * from_z + 16 * x, 16)
        for kk in (0, 1):
            await_bytes(gathered.at[kk, came], tok_recv.at[from_z, kk])
            for dx in (2, 1, 3):
                send(gathered.at[kk, came], gathered.at[kk, came], fwd_send, fwd_recv, to_x(around_x[dx]))
    waits.owe("fwd_send", gathered.at[:, pl.ds(0, 192)], fwd_send)
    waits.owe("fwd_recv", gathered.at[:, pl.ds(0, 192)], fwd_recv)

    waits.take(("share_recv", 0))
    for kk in (0, 1):
        fields[kk, 64:128, :] = jnp.zeros((64, 768), BF16)
        fields[kk, 0:64, 0:384] = table[kk, 0]
        fields[kk, 0:64, 384:768] = table[kk, 1]
    gate_mod = jnp.dot(onehot.astype(BF16)[:, 0:64], table[k, 2], preferred_element_type=F32)
    source = lax.broadcasted_iota(jnp.int32, (128, 256), 0)
    target = lax.broadcasted_iota(jnp.int32, (128, 256), 1)
    picks[...] = jnp.where(
        ((target < 128) & (source >= 64) & (source < 67)) | ((target >= 128) & (source >= 67) & (source < 70)), 1.0, 0.0
    ).astype(BF16)

    waits.take("fwd_recv")
    waits.take("stat_recv")

    table_of = stats[...]
    moments = jnp.dot(table_of, picks[...], preferred_element_type=F32)
    for kk in (0, 1):
        mods = jnp.dot(table_of, fields[kk], preferred_element_type=F32)
        for part_of in range(3):
            at = slice(128 * part_of, 128 * part_of + 128)
            after = slice(384 + 128 * part_of, 512 + 128 * part_of)
            normed[:, 384 * kk + 128 * part_of : 384 * kk + 128 * part_of + 128] = (
                (gathered[kk, :, at].astype(F32) - moments[:, 0:128]) * moments[:, 128:256] * (1.0 + mods[:, after])
                + mods[:, at]
            ).astype(BF16)

    def of_y(target):
        return pl.ds(pl.multiple_of(32 * target, 32), 32)

    routes = ((-4, -2), (-3, -1), (3, 1), (-1, -1), (1, 1))

    def send_part(n, slot):
        goal, via = routes[slot]
        send(part.at[n, of_y(at_y(goal))], part_in.at[n, slot], part_send, part_recv.at[n, slot], to_y(at_y(via)))
        waits.owe(("part", n, slot), part_in.at[n, slot], part_recv.at[n, slot])

    for n in range(2):
        waits.take(("share_recv", 1 + n))
        at = slice(512 * n, 512 * n + 512)
        part[n] = jnp.dot(normed[...], w1[:, at], preferred_element_type=F32).astype(BF16)
        for slot in (0, 1, 2):
            send_part(n, slot)
    for n in range(2):
        for slot in (3, 4):
            send_part(n, slot)
    for n in range(2):
        waits.take(("part", n, 2))
        relay[n, 1] = (part[n, of_y(at_y(2)), :].astype(F32) + part_in[n, 2].astype(F32)).astype(BF16)
        send(relay.at[n, 1], part_in.at[n, 6], part_send, part_recv.at[n, 6], to_y(at_y(2)))
        waits.take(("part", n, 1), ("part", n, 0))
        relay[n, 0] = (
            part[n, of_y(at_y(-2)), :].astype(F32) + part_in[n, 1].astype(F32) + part_in[n, 0].astype(F32)
        ).astype(BF16)
        send(relay.at[n, 0], part_in.at[n, 5], part_send, part_recv.at[n, 5], to_y(at_y(-2)))
        waits.owe(("part", n, 5), part_in.at[n, 5], part_recv.at[n, 5])
        waits.owe(("part", n, 6), part_in.at[n, 6], part_recv.at[n, 6])
    waits.owe("part_send", part_in, part_send)
    waits.take("sum_send", "tok_send", "fwd_send", "stat_send", "share_send")
    waits.take(("share_recv", 3))
    for n in range(2):
        waits.take(("part", n, 3), ("part", n, 4), ("part", n, 6), ("part", n, 5))

    mine = of_y(y)
    gate, up = (part[n, mine, :].astype(F32) + jnp.sum(part_in[n, 3:7].astype(F32), axis=0) for n in range(2))
    hidden[mine, :] = (gate / (1.0 + jnp.exp(-gate)) * up).astype(BF16)
    for slot, step in enumerate((2, -2, 1, -1)):
        send(hidden.at[mine], hidden.at[mine], hid_send, hid_recv.at[min(slot, 2)], to_y(at_y(step)))
    waits.owe("hid_a", hidden.at[pl.ds(0, 32)], hid_recv.at[0])
    waits.owe("hid_b", hidden.at[pl.ds(0, 32)], hid_recv.at[1])
    waits.take("part_send")
    waits.take("hid_a")
    came = of_y(at_y(-2))
    send(hidden.at[came], hidden.at[came], hid_send, hid_recv.at[2], to_y(at_y(2)))
    send(hidden.at[came], hidden.at[came], hid_send, hid_recv.at[2], to_y(at_y(1)))
    waits.take("hid_b")
    came = of_y(at_y(2))
    send(hidden.at[came], hidden.at[came], hid_send, hid_recv.at[2], to_y(at_y(-1)))
    waits.owe("hid_send", hidden.at[pl.ds(0, 224)], hid_send)
    waits.owe("hid_rest", hidden.at[pl.ds(0, 160)], hid_recv.at[2])
    waits.take("hid_rest")

    for kk in (0, 1):
        share = jnp.dot(hidden[...], w2[kk], preferred_element_type=F32).astype(BF16)
        for to_z in range(4):
            for goal_x in range(NX):
                at = 64 * to_z + 16 * goal_x
                down[to_z, goal_x, kk] = share[at : at + 16, :]
    far_first = near_first[::-1]
    for i, to_z in enumerate(far_first):
        send(down.at[to_z, at_x(2)], down_in.at[i, 0], dx_send, dx_recv.at[i, 0], to_x(at_x(-1)))
        send(down.at[to_z, at_x(1)], down_in.at[i, 1], dx_send, dx_recv.at[i, 1], to_x(at_x(1)))
    waits.take("hid_send")
    for i, to_z in enumerate(far_first):
        await_bytes(down_in.at[i, 0], dx_recv.at[i, 0])
        down_relay[i] = (down[to_z, at_x(-1)].astype(F32) + down_in[i, 0].astype(F32)).astype(BF16)
        send(down_relay.at[i], down_in.at[i, 2], dx_send, dx_recv.at[i, 2], to_x(at_x(-1)))
    for i, to_z in enumerate(far_first):
        await_bytes(down_in.at[i, 1], dx_recv.at[i, 1])
        await_bytes(down_in.at[i, 2], dx_recv.at[i, 2])
        down_mid[i] = (down[to_z, x].astype(F32) + down_in[i, 1].astype(F32) + down_in[i, 2].astype(F32)).astype(BF16)
        if i < 3:
            for core in (0, 1):
                send(down_mid.at[i, core], branch_in.at[z], dz_send, dz_recv, place(y, core, 4 * k + to_z, x))

    send(down_mid.at[3, 1 - k], branch_in.at[z], dz_send, dz_recv, place(y, 1 - k, 4 * k + far_first[3], x))

    @pl.when(k == hz)
    def _():
        pltpu.make_async_copy(down_mid.at[3, k], branch_in.at[z], dz_recv).start()

    @pl.when(k != hz)
    def _():
        send(down_mid.at[3, k], branch_in.at[z], dz_send, dz_recv, place(y, k, 4 * k + far_first[3], x))

    waits.owe("dx_send", down_in, dx_send)
    waits.owe("dz_recv", branch_in, dz_recv)
    waits.owe("dz_send", branch_in.at[pl.ds(0, 7)], dz_send)
    waits.owe("dz_send", own, dz_send, k != hz)
    waits.take("dz_recv")
    branch = jnp.sum(branch_in[...].astype(F32), axis=0)
    out[...] = (own[...].astype(F32) + gate_mod * branch).astype(BF16)
    waits.take("dx_send", "dz_send")


def on_device(tokens, token_frame, noise_level, modulation, gate_weight, up_weight, down_weight):
    hbm = pl.BlockSpec(memory_space=pltpu.HBM)
    vmem, dma = pltpu.VMEM, pltpu.SemaphoreType.DMA
    return pl.pallas_call(
        kernel,
        out_shape=jax.ShapeDtypeStruct((16, 384), BF16),
        in_specs=[hbm, hbm, hbm, hbm, hbm, hbm, hbm],
        out_specs=pl.BlockSpec(memory_space=pltpu.VMEM),
        scratch_shapes=[
            vmem((16, 384), BF16),
            vmem((2, 3, 64, 384), BF16),
            vmem((768, 1024), BF16),
            vmem((2, 512, 384), BF16),
            vmem((1, 1, 128), F32),
            vmem((16, 1, 128), F32),
            vmem((16, 128), BF16),
            vmem((256, 128), BF16),
            vmem((2, 256, 384), BF16),
            vmem((2, 128, 768), BF16),
            vmem((128, 256), BF16),
            vmem((256, 768), BF16),
            vmem((2, 256, 512), BF16),
            vmem((2, 7, 32, 512), BF16),
            vmem((2, 2, 32, 512), BF16),
            vmem((256, 512), BF16),
            vmem((4, 4, 2, 16, 384), BF16),
            vmem((4, 3, 2, 16, 384), BF16),
            vmem((4, 2, 16, 384), BF16),
            vmem((4, 2, 16, 384), BF16),
            vmem((8, 16, 384), BF16),
            pltpu.SMEM((2, 16), jnp.int32),
            dma((7,)),
            dma((4,)),
            dma((4,)),
            dma,
            dma,
            dma,
            dma((4, 2)),
            dma,
            dma,
            dma,
            dma,
            dma,
            dma((2, 7)),
            dma,
            dma((3,)),
            dma,
            dma((4, 3)),
            dma,
            dma,
        ],
        compiler_params=pltpu.CompilerParams(
            collective_id=0, has_side_effects=True, vmem_limit_bytes=60 << 20
        ),
        cost_estimate=pl.CostEstimate(flops=604_000_000, bytes_accessed=1_400_000, transcendentals=16384),
        name="modulated_feed_forward",
    )(tokens, token_frame, noise_level, jnp.transpose(modulation, (1, 0, 2)), gate_weight, up_weight, down_weight)


def solution(mesh):
    placed = (
        P("col", "row"),
        P("col"),
        P(),
        P(None, None, "row"),
        P("row", "col"),
        P("row", "col"),
        P("col", "row"),
    )
    return jax.shard_map(
        on_device, mesh=mesh, in_specs=placed, out_specs=P("col", "row"), check_vma=False
    )
```

```python
import jax
import jax.numpy as jnp
from jax import lax
from jax.experimental import pallas as pl
from jax.experimental.pallas import tpu as pltpu
from jax.sharding import PartitionSpec as P

D = 6144
EPS = 1e-06
NY, NZ, NX = 8, 8, 4
MESH = pl.DeviceIdType.MESH
F32, BF16 = jnp.float32, jnp.bfloat16


def place(y, core, z, x):
    return (y * 2 + core, z * NX + x)


def pieces(value):
    high = value.astype(BF16).astype(F32)
    rest = value - high
    middle = rest.astype(BF16).astype(F32)
    return high, middle, rest - middle


def in_lanes(lane, first, columns, base):
    for i, column in enumerate(columns):
        base = jnp.where(lane == first + i, column, base)
    return base


def send(src, dst, send_sem, recv_sem, device):
    pltpu.make_async_remote_copy(
        src, dst, send_sem, recv_sem, device_id=device, device_id_type=MESH
    ).start()


def await_bytes(ref, sem):
    pltpu.make_async_copy(ref, ref, sem).wait()


class Waits:
    def __init__(self):
        self.owed = {}

    def owe(self, name, ref, sem, when=None):
        self.owed.setdefault(name, []).append((ref, sem, when))

    def take(self, *names):
        for name in names:
            for ref, sem, when in self.owed.pop(name):
                if when is None:
                    await_bytes(ref, sem)
                else:
                    pl.when(when)(lambda ref=ref, sem=sem: await_bytes(ref, sem))


def kernel(
    tokens, frame, noise, modulation, gate_w, up_w, down_w, out,
    own, table, w1, w2, sum_out, sum_in, stat_out, stats, gathered, fields, picks,
    normed, part, part_in, relay, hidden, down, down_in, down_mid, branch_in, levels,
    local_sem, share_send, share_recv, sum_send, sum_recv, tok_send, tok_recv,
    fwd_send, fwd_recv, stat_send, stat_recv, part_send, part_recv, hid_send, hid_recv,
    dx_send, dx_recv, dz_send, dz_recv,
):
    row, col = lax.axis_index("row"), lax.axis_index("col")
    y, k, z, x = row // 2, row % 2, col // NX, col % NX
    hz = z // 4
    zz = z % 4
    way = 1 - 2 * k
    sibling = place(y, 1 - k, z, x)
    waits = Waits()

    def at_y(step, chunk):
        return lax.rem(y + 8 + (step if chunk == 0 else -step) * way, NY)

    def to_y(target):
        return place(target, k, z, x)

    def to_x(target):
        return place(y, k, z, target)

    upper = zz // 2
    outward = [zz, 1 - zz + 4 * upper, 2 - upper, 3 - 3 * upper]
    holds = 1 - (k - hz) * (k - hz)
    near_first = [outward[i] * holds + outward[3 - i] * (1 - holds) for i in range(4)]
    around_z = {dz: lax.rem(z + dz, NZ) for dz in range(1, NZ)}
    around_y = {dy: lax.rem(y + dy, NY) for dy in range(NY)}
    around_x = {dx: lax.rem(x + dx, NX) for dx in range(1, NX)}
    far_z, far_y = (4, 3, 5, 2, 6, 1, 7), (4, 3, 5, 2, 6, 1, 7, 0)

    own_copy = pltpu.make_async_copy(tokens, own, local_sem.at[0])
    own_copy.start()
    small = [
        pltpu.make_async_copy(frame, levels.at[0], local_sem.at[5]),
        pltpu.make_async_copy(noise, levels.at[1], local_sem.at[6]),
    ]
    for copy in small:
        copy.start()
    barrier = pltpu.get_barrier_semaphore()
    peers = [place(y, core, around_z[dz], x) for dz in far_z for core in (k, 1 - k)]
    peers += [place(around_y[dy], core, z, x) for dy in far_y for core in (k, 1 - k)][:-2] + [sibling]
    peers += [to_x(around_x[dx]) for dx in (2, 1, 3)]
    for peer in peers:
        pl.semaphore_signal(barrier, inc=1, device_id=peer, device_id_type=MESH)
    for i in range(4):
        from_z = 4 * k + i

        @pl.when(from_z != z)
        def _(from_z=from_z):
            for dx in (2, 1, 3):
                pl.semaphore_signal(barrier, inc=1, device_id=place(y, k, from_z, around_x[dx]), device_id_type=MESH)

    own_copy.wait()
    wide = own[...].astype(F32)
    lane = lax.broadcasted_iota(jnp.int32, (16, 128), 1)
    sublane = lax.broadcasted_iota(jnp.int32, (16, 128), 0)
    zero = jnp.zeros((16, 128), F32)
    square = jnp.sum(wide * wide, axis=1, keepdims=True)
    spread_out = jnp.where(lane == sublane, jnp.sum(wide, axis=1, keepdims=True), zero)
    spread_out = jnp.where(lane == sublane + 16, square, spread_out)
    sums = jnp.sum(spread_out, axis=0, keepdims=True)
    sum_out[0] = sums
    sum_in[row] = sums

    pl.semaphore_wait(barrier, len(peers) + 21 * holds)

    block = pl.ds(64 * zz + 16 * x, 16)
    for dz in (4, 3, 5, 2, 6, 1, 7):
        send(own, gathered.at[k, block], tok_send, tok_recv.at[zz, k], place(y, hz, around_z[dz], x))

    @pl.when(k == hz)
    def _():
        pltpu.make_async_copy(own, gathered.at[k, block], tok_recv.at[zz, k]).start()

    @pl.when(k != hz)
    def _():
        send(own, gathered.at[k, block], tok_send, tok_recv.at[zz, k], sibling)

    waits.owe("tok_send", gathered.at[0, pl.ds(0, 112)], tok_send)
    waits.owe("tok_send", own, tok_send, k != hz)

    for dy in far_y:
        for core in (k, 1 - k) if dy else (1 - k,):
            send(sum_out.at[0], sum_in.at[row], sum_send, sum_recv, place(around_y[dy], core, z, x))
    waits.owe("sum_send", sum_in.at[pl.ds(0, 15)], sum_send)
    waits.owe("sum_recv", sum_in.at[pl.ds(0, 15)], sum_recv)

    half = w1.at[pl.ds(0, 384), pl.ds(0, 512)]
    rows = pl.ds(384 * k, 384)
    for i, (source, goal, like) in enumerate(
        (
            (modulation, table.at[k], table.at[0]),
            (gate_w, w1.at[rows, pl.ds(0, 512)], half),
            (up_w, w1.at[rows, pl.ds(512, 512)], half),
            (down_w, w2.at[k], w2.at[0]),
        )
    ):
        pltpu.make_async_copy(source, goal, local_sem.at[1 + i]).start()
        send(source, goal, share_send.at[i], share_recv.at[i], sibling)
        waits.owe("share_send", like, share_send.at[i])
        waits.owe(("share_recv", i), like, share_recv.at[i])
        waits.owe(("share_recv", i), like, local_sem.at[1 + i])

    for copy in small:
        copy.wait()
    onehot = zero
    for t in range(16):
        level = levels[1, levels[0, t]]
        onehot = jnp.where((sublane == t) & (lane == level), 1.0, onehot)

    waits.take("sum_recv")
    total = jnp.broadcast_to(jnp.sum(sum_in[:, 0, :], axis=0, keepdims=True), (16, 128))
    center = jnp.sum(jnp.where(lane == sublane, total, zero), axis=1, keepdims=True) / D
    square = jnp.sum(jnp.where(lane == sublane + 16, total, zero), axis=1, keepdims=True) / D
    scale = lax.rsqrt(square - center * center + EPS)
    stat_out[...] = in_lanes(lane, 64, pieces(center) + pieces(scale), onehot).astype(BF16)

    @pl.when(k == hz)
    def _():
        for dz in far_z:
            for to in (around_x[2], around_x[1], around_x[3], x):
                send(stat_out, stats.at[block], stat_send, stat_recv.at[zz], place(y, k, around_z[dz], to))
        for dx in (2, 1, 3):
            send(stat_out, stats.at[block], stat_send, stat_recv.at[zz], to_x(around_x[dx]))
        pltpu.make_async_copy(stat_out, stats.at[block], stat_recv.at[zz]).start()

    waits.owe("stat_send", stats.at[pl.ds(0, 240)], stat_send, k == hz)
    waits.owe("stat_send", stats, stat_send, k == hz)
    for i in range(4):
        waits.owe(("stat_recv", i), stats.at[pl.ds(0, 64)], stat_recv.at[near_first[i]])

    for from_z in near_first:
        came = pl.ds(64 * from_z + 16 * x, 16)
        for kk in (0, 1):
            await_bytes(gathered.at[kk, came], tok_recv.at[from_z, kk])
            for dx in (2, 1, 3):
                send(gathered.at[kk, came], gathered.at[kk, came], fwd_send, fwd_recv.at[from_z], to_x(around_x[dx]))
    waits.owe("fwd_send", gathered.at[:, pl.ds(0, 192)], fwd_send)
    for i in range(4):
        waits.owe(("fwd_recv", i), gathered.at[:, pl.ds(0, 48)], fwd_recv.at[near_first[i]])

    waits.take(("share_recv", 0))
    for kk in (0, 1):
        fields[kk, 64:128, :] = jnp.zeros((64, 768), BF16)
        fields[kk, 0:64, 0:384] = table[kk, 0]
        fields[kk, 0:64, 384:768] = table[kk, 1]
    gate_mod = jnp.dot(onehot.astype(BF16)[:, 0:64], table[k, 2], preferred_element_type=F32)
    source = lax.broadcasted_iota(jnp.int32, (128, 256), 0)
    target = lax.broadcasted_iota(jnp.int32, (128, 256), 1)
    picks[...] = jnp.where(
        ((target < 128) & (source >= 64) & (source < 67)) | ((target >= 128) & (source >= 67) & (source < 70)), 1.0, 0.0
    ).astype(BF16)


    def of_y(target):
        return pl.ds(pl.multiple_of(16 * target, 16), 16)

    routes = ((-4, -2), (-3, -1), (3, 1), (-1, -1), (1, 1))
    for g in range(2):
        for b in range(2):
            i = 2 * g + b
            rows = pl.ds(pl.multiple_of(64 * near_first[i], 64), 64)
            waits.take(("fwd_recv", i), ("stat_recv", i))
            lookup = stats[rows, :]
            moments = jnp.dot(lookup, picks[...], preferred_element_type=F32)
            for kk in (0, 1):
                mods = jnp.dot(lookup, fields[kk], preferred_element_type=F32)
                for part_of in range(3):
                    at = slice(128 * part_of, 128 * part_of + 128)
                    after = slice(384 + 128 * part_of, 512 + 128 * part_of)
                    goal_at = slice(384 * kk + 128 * part_of, 384 * kk + 128 * part_of + 128)
                    normed[g, 64 * b : 64 * b + 64, goal_at] = (
                        (gathered[kk, rows, at].astype(F32) - moments[:, 0:128])
                        * moments[:, 128:256]
                        * (1.0 + mods[:, after])
                        + mods[:, at]
                    ).astype(BF16)
        if g == 0:
            waits.take(("share_recv", 1), ("share_recv", 2))
        part[g] = jnp.dot(normed[g], w1[...], preferred_element_type=F32).astype(BF16)
        for slot, (goal, via) in enumerate(routes):
            send(part.at[g, of_y(at_y(goal, g))], part_in.at[g, slot], part_send, part_recv.at[g, slot], to_y(at_y(via, g)))
            waits.owe(("part", g, slot), part_in.at[g, slot], part_recv.at[g, slot])
    for g in range(2):
        waits.take(("part", g, 2))
        relay[g, 1] = (part[g, of_y(at_y(2, g)), :].astype(F32) + part_in[g, 2].astype(F32)).astype(BF16)
        send(relay.at[g, 1], part_in.at[g, 6], part_send, part_recv.at[g, 6], to_y(at_y(2, g)))
        waits.take(("part", g, 1), ("part", g, 0))
        relay[g, 0] = (
            part[g, of_y(at_y(-2, g)), :].astype(F32) + part_in[g, 1].astype(F32) + part_in[g, 0].astype(F32)
        ).astype(BF16)
        send(relay.at[g, 0], part_in.at[g, 5], part_send, part_recv.at[g, 5], to_y(at_y(-2, g)))
        waits.owe(("part", g, 5), part_in.at[g, 5], part_recv.at[g, 5])
        waits.owe(("part", g, 6), part_in.at[g, 6], part_recv.at[g, 6])
    waits.owe("part_send", part_in, part_send)
    mine = of_y(y)
    for g in range(2):
        waits.take(("part", g, 3), ("part", g, 4), ("part", g, 6), ("part", g, 5))
        gate_up = part[g, mine, :].astype(F32) + jnp.sum(part_in[g, 3:7].astype(F32), axis=0)
        gate, up = gate_up[:, 0:512], gate_up[:, 512:1024]
        hidden[g, mine, :] = (gate / (1.0 + jnp.exp(-gate)) * up).astype(BF16)
        for dy in far_y[:-1]:
            send(hidden.at[g, mine], hidden.at[g, mine], hid_send, hid_recv.at[g], to_y(around_y[dy]))
        waits.owe(("hidden", g), hidden.at[0, pl.ds(0, 112)], hid_recv.at[g])
    waits.owe("hid_send", hidden.at[:, pl.ds(0, 112)], hid_send)
    waits.take("sum_send", "tok_send", "fwd_send", "stat_send", "share_send", "part_send")
    waits.take(("share_recv", 3))

    for g in range(2):
        waits.take(("hidden", g))
        for kk in (0, 1):
            share = jnp.dot(hidden[g], w2[kk], preferred_element_type=F32).astype(BF16)
            for b in range(2):
                for goal_x in range(NX):
                    at = 64 * b + 16 * goal_x
                    down[2 * g + b, goal_x, kk] = share[at : at + 16, :]
        for i in (2 * g + 1, 2 * g):
            for dx in (2, 1, 3):
                to = around_x[dx]
                send(down.at[i, to], down_in.at[i, dx - 1], dx_send, dx_recv.at[i], to_x(to))
            waits.owe(("down", i), down_in.at[i], dx_recv.at[i])
    waits.owe("dx_send", down_in, dx_send)
    for i in (1, 0, 3, 2):
        waits.take(("down", i))
        for kk in (0, 1):
            down_mid[i, kk] = (
                down[i, x, kk].astype(F32) + jnp.sum(down_in[i, :, kk].astype(F32), axis=0)
            ).astype(BF16)
        goal = 4 * k + near_first[i]
        if i:
            for core in (0, 1):
                send(down_mid.at[i, core], branch_in.at[z], dz_send, dz_recv, place(y, core, goal, x))
        else:
            send(down_mid.at[0, 1 - k], branch_in.at[z], dz_send, dz_recv, place(y, 1 - k, goal, x))

            @pl.when(k == hz)
            def _():
                pltpu.make_async_copy(down_mid.at[0, k], branch_in.at[z], dz_recv).start()

            @pl.when(k != hz)
            def _(goal=goal):
                send(down_mid.at[0, k], branch_in.at[z], dz_send, dz_recv, place(y, k, goal, x))

    waits.owe("dz_recv", branch_in, dz_recv)
    waits.owe("dz_send", branch_in.at[pl.ds(0, 7)], dz_send)
    waits.owe("dz_send", own, dz_send, k != hz)
    waits.take("hid_send", "dz_recv")
    branch = jnp.sum(branch_in[...].astype(F32), axis=0)
    out[...] = (own[...].astype(F32) + gate_mod * branch).astype(BF16)
    waits.take("dx_send", "dz_send")


def on_device(tokens, token_frame, noise_level, modulation, gate_weight, up_weight, down_weight):
    hbm = pl.BlockSpec(memory_space=pltpu.HBM)
    vmem, dma = pltpu.VMEM, pltpu.SemaphoreType.DMA
    return pl.pallas_call(
        kernel,
        out_shape=jax.ShapeDtypeStruct((16, 384), BF16),
        in_specs=[hbm, hbm, hbm, hbm, hbm, hbm, hbm],
        out_specs=pl.BlockSpec(memory_space=pltpu.VMEM),
        scratch_shapes=[
            vmem((16, 384), BF16),
            vmem((2, 3, 64, 384), BF16),
            vmem((768, 1024), BF16),
            vmem((2, 512, 384), BF16),
            vmem((1, 1, 128), F32),
            vmem((16, 1, 128), F32),
            vmem((16, 128), BF16),
            vmem((256, 128), BF16),
            vmem((2, 256, 384), BF16),
            vmem((2, 128, 768), BF16),
            vmem((128, 256), BF16),
            vmem((2, 128, 768), BF16),
            vmem((2, 128, 1024), BF16),
            vmem((2, 7, 16, 1024), BF16),
            vmem((2, 2, 16, 1024), BF16),
            vmem((2, 128, 512), BF16),
            vmem((4, 4, 2, 16, 384), BF16),
            vmem((4, 3, 2, 16, 384), BF16),
            vmem((4, 2, 16, 384), BF16),
            vmem((8, 16, 384), BF16),
            pltpu.SMEM((2, 16), jnp.int32),
            dma((7,)),
            dma((4,)),
            dma((4,)),
            dma,
            dma,
            dma,
            dma((4, 2)),
            dma,
            dma((4,)),
            dma,
            dma((4,)),
            dma,
            dma((2, 7)),
            dma,
            dma((2,)),
            dma,
            dma((4,)),
            dma,
            dma,
        ],
        compiler_params=pltpu.CompilerParams(
            collective_id=0, has_side_effects=True, vmem_limit_bytes=60 << 20
        ),
        cost_estimate=pl.CostEstimate(flops=604_000_000, bytes_accessed=1_400_000, transcendentals=16384),
        name="modulated_feed_forward",
    )(tokens, token_frame, noise_level, jnp.transpose(modulation, (1, 0, 2)), gate_weight, up_weight, down_weight)


def solution(mesh):
    placed = (
        P("col", "row"),
        P("col"),
        P(),
        P(None, None, "row"),
        P("row", "col"),
        P("row", "col"),
        P("col", "row"),
    )
    return jax.shard_map(
        on_device, mesh=mesh, in_specs=placed, out_specs=P("col", "row"), check_vma=False
    )
```

```python
import jax
import jax.numpy as jnp
from jax import lax
from jax.experimental import pallas as pl
from jax.experimental.pallas import tpu as pltpu
from jax.sharding import PartitionSpec as P

D = 6144
EPS = 1e-06
NY, NZ, NX = 8, 8, 4
MESH = pl.DeviceIdType.MESH
F32, BF16 = jnp.float32, jnp.bfloat16


def place(y, core, z, x):
    return (y * 2 + core, z * NX + x)


def pieces(value):
    high = value.astype(BF16).astype(F32)
    rest = value - high
    middle = rest.astype(BF16).astype(F32)
    return high, middle, rest - middle


def in_lanes(lane, first, columns, base):
    for i, column in enumerate(columns):
        base = jnp.where(lane == first + i, column, base)
    return base


def send(src, dst, send_sem, recv_sem, device):
    pltpu.make_async_remote_copy(
        src, dst, send_sem, recv_sem, device_id=device, device_id_type=MESH
    ).start()


def await_bytes(ref, sem):
    pltpu.make_async_copy(ref, ref, sem).wait()


class Waits:
    def __init__(self):
        self.owed = {}

    def owe(self, name, ref, sem, when=None):
        self.owed.setdefault(name, []).append((ref, sem, when))

    def take(self, *names):
        for name in names:
            for ref, sem, when in self.owed.pop(name):
                if when is None:
                    await_bytes(ref, sem)
                else:
                    pl.when(when)(lambda ref=ref, sem=sem: await_bytes(ref, sem))


def kernel(
    tokens, frame, noise, modulation, gate_w, up_w, down_w, out,
    own, table, w1, w2, sum_out, sum_in, stat_out, stats, gathered, fields, picks,
    normed, part, part_in, relay, hidden, down, down_in, down_mid, branch_in, levels,
    local_sem, share_send, share_recv, sum_send, sum_recv, tok_send, tok_recv,
    fwd_send, fwd_recv, stat_send, stat_recv, part_send, part_recv, hid_send, hid_recv,
    dx_send, dx_recv, dz_send, dz_recv, ready,
):
    row, col = lax.axis_index("row"), lax.axis_index("col")
    y, k, z, x = row // 2, row % 2, col // NX, col % NX
    hz = z // 4
    zz = z % 4
    way = 1 - 2 * k
    sibling = place(y, 1 - k, z, x)
    waits = Waits()

    def at_y(step, chunk):
        return lax.rem(y + 8 + (step if chunk == 0 else -step) * way, NY)

    def to_y(target):
        return place(target, k, z, x)

    def to_x(target):
        return place(y, k, z, target)

    upper = zz // 2
    outward = [zz, 1 - zz + 4 * upper, 2 - upper, 3 - 3 * upper]
    holds = 1 - (k - hz) * (k - hz)
    near_first = [outward[i] * holds + outward[3 - i] * (1 - holds) for i in range(4)]
    around_z = {dz: lax.rem(z + dz, NZ) for dz in range(1, NZ)}
    around_y = {dy: lax.rem(y + dy, NY) for dy in range(NY)}
    around_x = {dx: lax.rem(x + dx, NX) for dx in range(1, NX)}
    far_z, far_y = (4, 3, 5, 2, 6, 1, 7), (4, 3, 5, 2, 6, 1, 7, 0)

    own_copy = pltpu.make_async_copy(tokens, own, local_sem.at[0])
    own_copy.start()
    small = [
        pltpu.make_async_copy(frame, levels.at[0], local_sem.at[5]),
        pltpu.make_async_copy(noise, levels.at[1], local_sem.at[6]),
    ]
    for copy in small:
        copy.start()
    barrier = pltpu.get_barrier_semaphore()

    def enter(device):
        pl.semaphore_signal(barrier, inc=1, device_id=device, device_id_type=MESH)

    for dz in far_z:
        enter(place(y, 1, around_z[dz], x))
    for i in range(4):
        from_z = 4 * k + i

        @pl.when(from_z != z)
        def _(from_z=from_z):
            for dx in (2, 1, 3):
                enter(place(y, 1, from_z, around_x[dx]))

    for dy in far_y[:-1]:
        enter(place(around_y[dy], 0, z, x))
    for dx in (2, 1, 3):
        enter(place(y, 0, z, around_x[dx]))
    enter(sibling)

    own_copy.wait()
    wide = own[...].astype(F32)
    lane = lax.broadcasted_iota(jnp.int32, (16, 128), 1)
    sublane = lax.broadcasted_iota(jnp.int32, (16, 128), 0)
    zero = jnp.zeros((16, 128), F32)
    square = jnp.sum(wide * wide, axis=1, keepdims=True)
    spread_out = jnp.where(lane == sublane, jnp.sum(wide, axis=1, keepdims=True), zero)
    spread_out = jnp.where(lane == sublane + 16, square, spread_out)
    sums = jnp.sum(spread_out, axis=0, keepdims=True)
    sum_out[0] = sums
    sum_in[row] = sums

    @pl.when(k == 0)
    def _():
        pl.semaphore_wait(barrier, 21)
        pl.semaphore_signal(ready.at[0], inc=1, device_id=sibling, device_id_type=MESH)

    @pl.when(k == 1)
    def _():
        pl.semaphore_wait(ready.at[0], 1)

    for dy in far_y:
        for core in (k, 1 - k) if dy else (1 - k,):
            send(sum_out.at[0], sum_in.at[row], sum_send, sum_recv, place(around_y[dy], core, z, x))
    waits.owe("sum_send", sum_in.at[pl.ds(0, 15)], sum_send)
    waits.owe("sum_recv", sum_in.at[pl.ds(0, 15)], sum_recv)

    half = w1.at[pl.ds(0, 384), pl.ds(0, 512)]
    rows = pl.ds(384 * k, 384)
    for i, (source, goal, like) in enumerate(
        (
            (modulation, table.at[k], table.at[0]),
            (gate_w, w1.at[rows, pl.ds(0, 512)], half),
            (up_w, w1.at[rows, pl.ds(512, 512)], half),
            (down_w, w2.at[k], w2.at[0]),
        )
    ):
        pltpu.make_async_copy(source, goal, local_sem.at[1 + i]).start()
        send(source, goal, share_send.at[i], share_recv.at[i], sibling)
        waits.owe("share_send", like, share_send.at[i])
        waits.owe(("share_recv", i), like, share_recv.at[i])
        waits.owe(("share_recv", i), like, local_sem.at[1 + i])

    @pl.when(k == 1)
    def _():
        pl.semaphore_wait(barrier, 36)
        pl.semaphore_signal(ready.at[1], inc=1, device_id=sibling, device_id_type=MESH)

    @pl.when(k == 0)
    def _():
        pl.semaphore_wait(ready.at[1], 1)

    block = pl.ds(64 * zz + 16 * x, 16)
    for dz in (4, 3, 5, 2, 6, 1, 7):
        send(own, gathered.at[k, block], tok_send, tok_recv.at[zz, k], place(y, hz, around_z[dz], x))

    @pl.when(k == hz)
    def _():
        pltpu.make_async_copy(own, gathered.at[k, block], tok_recv.at[zz, k]).start()

    @pl.when(k != hz)
    def _():
        send(own, gathered.at[k, block], tok_send, tok_recv.at[zz, k], sibling)

    waits.owe("tok_send", gathered.at[0, pl.ds(0, 112)], tok_send)
    waits.owe("tok_send", own, tok_send, k != hz)

    for copy in small:
        copy.wait()
    onehot = zero
    for t in range(16):
        level = levels[1, levels[0, t]]
        onehot = jnp.where((sublane == t) & (lane == level), 1.0, onehot)

    waits.take("sum_recv")
    total = jnp.broadcast_to(jnp.sum(sum_in[:, 0, :], axis=0, keepdims=True), (16, 128))
    center = jnp.sum(jnp.where(lane == sublane, total, zero), axis=1, keepdims=True) / D
    square = jnp.sum(jnp.where(lane == sublane + 16, total, zero), axis=1, keepdims=True) / D
    scale = lax.rsqrt(square - center * center + EPS)
    stat_out[...] = in_lanes(lane, 64, pieces(center) + pieces(scale), onehot).astype(BF16)

    @pl.when(k == hz)
    def _():
        for dz in far_z:
            for to in (around_x[2], around_x[1], around_x[3], x):
                send(stat_out, stats.at[block], stat_send, stat_recv.at[zz], place(y, k, around_z[dz], to))
        for dx in (2, 1, 3):
            send(stat_out, stats.at[block], stat_send, stat_recv.at[zz], to_x(around_x[dx]))
        pltpu.make_async_copy(stat_out, stats.at[block], stat_recv.at[zz]).start()

    waits.owe("stat_send", stats.at[pl.ds(0, 240)], stat_send, k == hz)
    waits.owe("stat_send", stats, stat_send, k == hz)
    for i in range(4):
        waits.owe(("stat_recv", i), stats.at[pl.ds(0, 64)], stat_recv.at[near_first[i]])

    for from_z in near_first:
        came = pl.ds(64 * from_z + 16 * x, 16)
        for kk in (0, 1):
            await_bytes(gathered.at[kk, came], tok_recv.at[from_z, kk])
            for dx in (2, 1, 3):
                send(gathered.at[kk, came], gathered.at[kk, came], fwd_send, fwd_recv.at[from_z], to_x(around_x[dx]))
    waits.owe("fwd_send", gathered.at[:, pl.ds(0, 192)], fwd_send)
    for i in range(4):
        waits.owe(("fwd_recv", i), gathered.at[:, pl.ds(0, 48)], fwd_recv.at[near_first[i]])

    waits.take(("share_recv", 0))
    for kk in (0, 1):
        fields[kk, 64:128, :] = jnp.zeros((64, 768), BF16)
        fields[kk, 0:64, 0:384] = table[kk, 0]
        fields[kk, 0:64, 384:768] = table[kk, 1]
    gate_mod = jnp.dot(onehot.astype(BF16)[:, 0:64], table[k, 2], preferred_element_type=F32)
    source = lax.broadcasted_iota(jnp.int32, (128, 256), 0)
    target = lax.broadcasted_iota(jnp.int32, (128, 256), 1)
    picks[...] = jnp.where(
        ((target < 128) & (source >= 64) & (source < 67)) | ((target >= 128) & (source >= 67) & (source < 70)), 1.0, 0.0
    ).astype(BF16)


    def of_y(target):
        return pl.ds(pl.multiple_of(16 * target, 16), 16)

    routes = ((-4, -2), (-3, -1), (3, 1), (-1, -1), (1, 1))
    for g in range(2):
        for b in range(2):
            i = 2 * g + b
            rows = pl.ds(pl.multiple_of(64 * near_first[i], 64), 64)
            waits.take(("fwd_recv", i), ("stat_recv", i))
            lookup = stats[rows, :]
            moments = jnp.dot(lookup, picks[...], preferred_element_type=F32)
            for kk in (0, 1):
                mods = jnp.dot(lookup, fields[kk], preferred_element_type=F32)
                for part_of in range(3):
                    at = slice(128 * part_of, 128 * part_of + 128)
                    after = slice(384 + 128 * part_of, 512 + 128 * part_of)
                    goal_at = slice(384 * kk + 128 * part_of, 384 * kk + 128 * part_of + 128)
                    normed[g, 64 * b : 64 * b + 64, goal_at] = (
                        (gathered[kk, rows, at].astype(F32) - moments[:, 0:128])
                        * moments[:, 128:256]
                        * (1.0 + mods[:, after])
                        + mods[:, at]
                    ).astype(BF16)
        if g == 0:
            waits.take(("share_recv", 1), ("share_recv", 2))
        part[g] = jnp.dot(normed[g], w1[...], preferred_element_type=F32).astype(BF16)
        for slot, (goal, via) in enumerate(routes):
            send(part.at[g, of_y(at_y(goal, g))], part_in.at[g, slot], part_send, part_recv.at[g, slot], to_y(at_y(via, g)))
            waits.owe(("part", g, slot), part_in.at[g, slot], part_recv.at[g, slot])
    for g in range(2):
        waits.take(("part", g, 2))
        relay[g, 1] = (part[g, of_y(at_y(2, g)), :].astype(F32) + part_in[g, 2].astype(F32)).astype(BF16)
        send(relay.at[g, 1], part_in.at[g, 6], part_send, part_recv.at[g, 6], to_y(at_y(2, g)))
        waits.take(("part", g, 1), ("part", g, 0))
        relay[g, 0] = (
            part[g, of_y(at_y(-2, g)), :].astype(F32) + part_in[g, 1].astype(F32) + part_in[g, 0].astype(F32)
        ).astype(BF16)
        send(relay.at[g, 0], part_in.at[g, 5], part_send, part_recv.at[g, 5], to_y(at_y(-2, g)))
        waits.owe(("part", g, 5), part_in.at[g, 5], part_recv.at[g, 5])
        waits.owe(("part", g, 6), part_in.at[g, 6], part_recv.at[g, 6])
    waits.owe("part_send", part_in, part_send)
    mine = of_y(y)
    for g in range(2):
        waits.take(("part", g, 3), ("part", g, 4), ("part", g, 6), ("part", g, 5))
        gate_up = part[g, mine, :].astype(F32) + jnp.sum(part_in[g, 3:7].astype(F32), axis=0)
        gate, up = gate_up[:, 0:512], gate_up[:, 512:1024]
        hidden[g, mine, :] = (gate / (1.0 + jnp.exp(-gate)) * up).astype(BF16)
        for dy in far_y[:-1]:
            send(hidden.at[g, mine], hidden.at[g, mine], hid_send, hid_recv.at[g], to_y(around_y[dy]))
        waits.owe(("hidden", g), hidden.at[0, pl.ds(0, 112)], hid_recv.at[g])
    waits.owe("hid_send", hidden.at[:, pl.ds(0, 112)], hid_send)
    waits.take("sum_send", "tok_send", "fwd_send", "stat_send", "share_send", "part_send")
    waits.take(("share_recv", 3))

    for g in range(2):
        waits.take(("hidden", g))
        for kk in (0, 1):
            share = jnp.dot(hidden[g], w2[kk], preferred_element_type=F32).astype(BF16)
            for b in range(2):
                for goal_x in range(NX):
                    at = 64 * b + 16 * goal_x
                    down[2 * g + b, goal_x, kk] = share[at : at + 16, :]
        for i in (2 * g + 1, 2 * g):
            for dx in (2, 1, 3):
                to = around_x[dx]
                send(down.at[i, to], down_in.at[i, dx - 1], dx_send, dx_recv.at[i], to_x(to))
            waits.owe(("down", i), down_in.at[i], dx_recv.at[i])
    waits.owe("dx_send", down_in, dx_send)
    for i in (1, 0, 3, 2):
        waits.take(("down", i))
        for kk in (0, 1):
            down_mid[i, kk] = (
                down[i, x, kk].astype(F32) + jnp.sum(down_in[i, :, kk].astype(F32), axis=0)
            ).astype(BF16)
        goal = 4 * k + near_first[i]
        if i:
            for core in (0, 1):
                send(down_mid.at[i, core], branch_in.at[z], dz_send, dz_recv, place(y, core, goal, x))
        else:
            send(down_mid.at[0, 1 - k], branch_in.at[z], dz_send, dz_recv, place(y, 1 - k, goal, x))

            @pl.when(k == hz)
            def _():
                pltpu.make_async_copy(down_mid.at[0, k], branch_in.at[z], dz_recv).start()

            @pl.when(k != hz)
            def _(goal=goal):
                send(down_mid.at[0, k], branch_in.at[z], dz_send, dz_recv, place(y, k, goal, x))

    waits.owe("dz_recv", branch_in, dz_recv)
    waits.owe("dz_send", branch_in.at[pl.ds(0, 7)], dz_send)
    waits.owe("dz_send", own, dz_send, k != hz)
    waits.take("hid_send", "dz_recv")
    branch = jnp.sum(branch_in[...].astype(F32), axis=0)
    out[...] = (own[...].astype(F32) + gate_mod * branch).astype(BF16)
    waits.take("dx_send", "dz_send")


def on_device(tokens, token_frame, noise_level, modulation, gate_weight, up_weight, down_weight):
    hbm = pl.BlockSpec(memory_space=pltpu.HBM)
    vmem, dma = pltpu.VMEM, pltpu.SemaphoreType.DMA
    return pl.pallas_call(
        kernel,
        out_shape=jax.ShapeDtypeStruct((16, 384), BF16),
        in_specs=[hbm, hbm, hbm, hbm, hbm, hbm, hbm],
        out_specs=pl.BlockSpec(memory_space=pltpu.VMEM),
        scratch_shapes=[
            vmem((16, 384), BF16),
            vmem((2, 3, 64, 384), BF16),
            vmem((768, 1024), BF16),
            vmem((2, 512, 384), BF16),
            vmem((1, 1, 128), F32),
            vmem((16, 1, 128), F32),
            vmem((16, 128), BF16),
            vmem((256, 128), BF16),
            vmem((2, 256, 384), BF16),
            vmem((2, 128, 768), BF16),
            vmem((128, 256), BF16),
            vmem((2, 128, 768), BF16),
            vmem((2, 128, 1024), BF16),
            vmem((2, 7, 16, 1024), BF16),
            vmem((2, 2, 16, 1024), BF16),
            vmem((2, 128, 512), BF16),
            vmem((4, 4, 2, 16, 384), BF16),
            vmem((4, 3, 2, 16, 384), BF16),
            vmem((4, 2, 16, 384), BF16),
            vmem((8, 16, 384), BF16),
            pltpu.SMEM((2, 16), jnp.int32),
            dma((7,)),
            dma((4,)),
            dma((4,)),
            dma,
            dma,
            dma,
            dma((4, 2)),
            dma,
            dma((4,)),
            dma,
            dma((4,)),
            dma,
            dma((2, 7)),
            dma,
            dma((2,)),
            dma,
            dma((4,)),
            dma,
            dma,
            pltpu.SemaphoreType.REGULAR((2,)),
        ],
        compiler_params=pltpu.CompilerParams(
            collective_id=0, has_side_effects=True, vmem_limit_bytes=60 << 20
        ),
        cost_estimate=pl.CostEstimate(flops=604_000_000, bytes_accessed=1_400_000, transcendentals=16384),
        name="modulated_feed_forward",
    )(tokens, token_frame, noise_level, jnp.transpose(modulation, (1, 0, 2)), gate_weight, up_weight, down_weight)


def solution(mesh):
    placed = (
        P("col", "row"),
        P("col"),
        P(),
        P(None, None, "row"),
        P("row", "col"),
        P("row", "col"),
        P("col", "row"),
    )
    return jax.shard_map(
        on_device, mesh=mesh, in_specs=placed, out_specs=P("col", "row"), check_vma=False
    )
```

```python
import functools

import jax
import jax.numpy as jnp
from jax import lax
from jax.experimental import pallas as pl
from jax.experimental.pallas import tpu as pltpu
from jax.sharding import PartitionSpec as P

D = 6144
EPS = 1e-06
NY, NZ, NX = 8, 8, 4
MESH = pl.DeviceIdType.MESH
F32, BF16 = jnp.float32, jnp.bfloat16


def place(y, core, z, x):
    return (y * 2 + core, z * NX + x)


def pieces(value):
    high = value.astype(BF16).astype(F32)
    rest = value - high
    middle = rest.astype(BF16).astype(F32)
    return high, middle, rest - middle


def in_lanes(lane, first, columns, base):
    for i, column in enumerate(columns):
        base = jnp.where(lane == first + i, column, base)
    return base


def send(src, dst, send_sem, recv_sem, device):
    pltpu.make_async_remote_copy(
        src, dst, send_sem, recv_sem, device_id=device, device_id_type=MESH
    ).start()


def await_bytes(ref, sem):
    pltpu.make_async_copy(ref, ref, sem).wait()


class Waits:
    def __init__(self):
        self.owed = {}

    def owe(self, name, ref, sem, when=None):
        self.owed.setdefault(name, []).append((ref, sem, when))

    def take(self, *names):
        for name in names:
            for ref, sem, when in self.owed.pop(name):
                if when is None:
                    await_bytes(ref, sem)
                else:
                    pl.when(when)(lambda ref=ref, sem=sem: await_bytes(ref, sem))


def kernel(
    tokens, frame, noise, modulation, gate_w, up_w, down_w, out,
    own, table, w1, w2, sum_out, sum_in, stat_out, stats, gathered, fields, picks,
    normed, part, part_in, relay, hidden, down, down_in, down_mid, branch_in, levels,
    local_sem, share_send, share_recv, sum_send, sum_recv, tok_send, tok_recv,
    fwd_send, fwd_recv, stat_send, stat_recv, statf_recv, part_send, part_recv, hid_send, hid_recv,
    dx_send, dx_recv, dz_send, dz_recv, ready,
):
    row, col = lax.axis_index("row"), lax.axis_index("col")
    y, k, z, x = row // 2, row % 2, col // NX, col % NX
    hz = z // 4
    zz = z % 4
    way = 1 - 2 * k
    sibling = place(y, 1 - k, z, x)
    waits = Waits()

    def at_y(step, chunk):
        return lax.rem(y + 8 + (step if chunk == 0 else -step) * way, NY)

    def to_y(target):
        return place(target, k, z, x)

    def to_x(target):
        return place(y, k, z, target)

    upper = zz // 2
    outward = [zz, 1 - zz + 4 * upper, 2 - upper, 3 - 3 * upper]
    holds = 1 - (k - hz) * (k - hz)
    near_first = [outward[i] * holds + outward[3 - i] * (1 - holds) for i in range(4)]
    order = [i * (1 - k) + near_first[i] * k for i in range(4)]
    around_z = {dz: lax.rem(z + dz, NZ) for dz in range(1, NZ)}
    around_y = {dy: lax.rem(y + dy, NY) for dy in range(NY)}
    around_x = {dx: lax.rem(x + dx, NX) for dx in range(1, NX)}
    far_z, far_y = (4, 3, 5, 2, 6, 1, 7), (4, 3, 5, 2, 6, 1, 7, 0)

    own_copy = pltpu.make_async_copy(tokens, own, local_sem.at[0])
    own_copy.start()
    small = [
        pltpu.make_async_copy(frame, levels.at[0], local_sem.at[5]),
        pltpu.make_async_copy(noise, levels.at[1], local_sem.at[6]),
    ]
    for copy in small:
        copy.start()
    barrier = pltpu.get_barrier_semaphore()

    def enter(device):
        pl.semaphore_signal(barrier, inc=1, device_id=device, device_id_type=MESH)

    for dz in far_z:
        enter(place(y, 1, around_z[dz], x))
    @pl.when(k == 1)
    def _():
        for from_z in range(4, NZ):

            @pl.when(from_z != z)
            def _(from_z=from_z):
                for dx in (2, 1, 3):
                    enter(place(y, 1, from_z, around_x[dx]))

    for dy in far_y[:-1]:
        enter(place(around_y[dy], 0, z, x))
    for dx in (2, 1, 3):
        enter(place(y, 0, z, around_x[dx]))
    enter(sibling)

    own_copy.wait()
    wide = own[...].astype(F32)
    lane = lax.broadcasted_iota(jnp.int32, (16, 128), 1)
    sublane = lax.broadcasted_iota(jnp.int32, (16, 128), 0)
    zero = jnp.zeros((16, 128), F32)
    square = jnp.sum(wide * wide, axis=1, keepdims=True)
    spread_out = jnp.where(lane == sublane, jnp.sum(wide, axis=1, keepdims=True), zero)
    spread_out = jnp.where(lane == sublane + 16, square, spread_out)
    sums = jnp.sum(spread_out, axis=0, keepdims=True)
    sum_out[0] = sums
    sum_in[row] = sums

    @pl.when(k == 0)
    def _():
        pl.semaphore_wait(barrier, 21)
        pl.semaphore_signal(ready.at[0], inc=1, device_id=sibling, device_id_type=MESH)

    @pl.when(k == 1)
    def _():
        pl.semaphore_wait(ready.at[0], 1)

    for dy in far_y:
        for core in (k, 1 - k) if dy else (1 - k,):
            send(sum_out.at[0], sum_in.at[row], sum_send, sum_recv, place(around_y[dy], core, z, x))
    waits.owe("sum_send", sum_in.at[pl.ds(0, 15)], sum_send)
    waits.owe("sum_recv", sum_in.at[pl.ds(0, 15)], sum_recv)

    half = w1.at[pl.ds(0, 384), pl.ds(0, 512)]
    rows = pl.ds(384 * k, 384)
    shared = (
        (modulation, table.at[k], table.at[0]),
        (gate_w, w1.at[rows, pl.ds(0, 512)], half),
        (up_w, w1.at[rows, pl.ds(512, 512)], half),
        (down_w, w2.at[k], w2.at[0]),
    )
    for i, (_, _, like) in enumerate(shared):
        waits.owe("share_send", like, share_send.at[i])
        waits.owe(("share_recv", i), like, share_recv.at[i])
        waits.owe(("share_recv", i), like, local_sem.at[1 + i])

    def share():
        for i, (source, goal, _) in enumerate(shared):
            pltpu.make_async_copy(source, goal, local_sem.at[1 + i]).start()
            send(source, goal, share_send.at[i], share_recv.at[i], sibling)

    pl.when(hz == 0)(share)

    @pl.when(k == 1)
    def _():
        pl.semaphore_wait(barrier, 15 + 21 * hz)
        pl.semaphore_signal(ready.at[1], inc=1, device_id=sibling, device_id_type=MESH)

    @pl.when(k == 0)
    def _():
        pl.semaphore_wait(ready.at[1], 1)

    block = pl.ds(64 * zz + 16 * x, 16)
    for to_z in [4 * (1 - hz) + lax.rem(zz + d, 4) for d in (0, 1, 3, 2)] + [4 * hz + lax.rem(zz + d, 4) for d in (2, 1, 3)]:
        send(own, gathered.at[k, block], tok_send, tok_recv.at[zz, k], place(y, hz, to_z, x))

    @pl.when(k == hz)
    def _():
        pltpu.make_async_copy(own, gathered.at[k, block], tok_recv.at[zz, k]).start()

    @pl.when(k != hz)
    def _():
        send(own, gathered.at[k, block], tok_send, tok_recv.at[zz, k], sibling)

    waits.owe("tok_send", gathered.at[0, pl.ds(0, 112)], tok_send)
    waits.owe("tok_send", own, tok_send, k != hz)

    pl.when(hz == 1)(share)
    for copy in small:
        copy.wait()
    onehot = zero
    for t in range(16):
        level = levels[1, levels[0, t]]
        onehot = jnp.where((sublane == t) & (lane == level), 1.0, onehot)

    waits.take("sum_recv")
    total = jnp.broadcast_to(jnp.sum(sum_in[:, 0, :], axis=0, keepdims=True), (16, 128))
    center = jnp.sum(jnp.where(lane == sublane, total, zero), axis=1, keepdims=True) / D
    square = jnp.sum(jnp.where(lane == sublane + 16, total, zero), axis=1, keepdims=True) / D
    scale = lax.rsqrt(square - center * center + EPS)
    stat_out[...] = in_lanes(lane, 64, pieces(center) + pieces(scale), onehot).astype(BF16)

    @pl.when((k == 1) & (hz == 1))
    def _():
        for dz in far_z:
            for to in (around_x[2], around_x[1], around_x[3], x):
                send(stat_out, stats.at[block], stat_send, stat_recv.at[zz], place(y, k, around_z[dz], to))
        for dx in (2, 1, 3):
            send(stat_out, stats.at[block], stat_send, stat_recv.at[zz], to_x(around_x[dx]))
        pltpu.make_async_copy(stat_out, stats.at[block], stat_recv.at[zz]).start()

    @pl.when((k == 0) & (hz == 0))
    def _():
        for dz in far_z:
            send(stat_out, stats.at[block], stat_send, stat_recv.at[zz], place(y, k, around_z[dz], x))
        pltpu.make_async_copy(stat_out, stats.at[block], stat_recv.at[zz]).start()

    waits.owe("stat_send", stats, stat_send, (k == 1) & (hz == 1))
    waits.owe("stat_send", stats.at[pl.ds(0, 240)], stat_send, (k == 1) & (hz == 1))
    waits.owe("stat_send", stats.at[pl.ds(0, 112)], stat_send, (k == 0) & (hz == 0))
    waits.owe("stat_send", stats.at[pl.ds(0, 192)], stat_send, k == 0)

    def forward(like, from_z, send_sem, recv_sem):
        for dx in (2, 1, 3):
            send(like, like, send_sem, recv_sem.at[from_z], to_x(around_x[dx]))

    def forward_stats(from_z):
        came = stats.at[pl.ds(64 * from_z + 16 * x, 16)]
        await_bytes(came, stat_recv.at[from_z])
        forward(came, from_z, stat_send, statf_recv)

    for i, from_z in enumerate(near_first):
        for kk in (0, 1):
            came = gathered.at[kk, pl.ds(64 * from_z + 16 * x, 16)]
            await_bytes(came, tok_recv.at[from_z, kk])
            forward(came, from_z, fwd_send, fwd_recv)
        if i % 2:
            for near in near_first[i - 1 : i + 1]:
                pl.when(k == 0)(functools.partial(forward_stats, near))
    for i in range(4):
        waits.owe(("stat_recv", i), stats.at[pl.ds(0, 48)], statf_recv.at[order[i]], k == 0)
        waits.owe(("stat_recv", i), stats.at[pl.ds(0, 64)], stat_recv.at[order[i]], k == 1)
    waits.owe("fwd_send", gathered.at[:, pl.ds(0, 192)], fwd_send)
    for i in range(4):
        waits.owe(("fwd_recv", i), gathered.at[:, pl.ds(0, 48)], fwd_recv.at[order[i]])

    waits.take(("share_recv", 0))
    for kk in (0, 1):
        fields[kk, 64:128, :] = jnp.zeros((64, 768), BF16)
        fields[kk, 0:64, 0:384] = table[kk, 0]
        fields[kk, 0:64, 384:768] = table[kk, 1]
    gate_mod = jnp.dot(onehot.astype(BF16)[:, 0:64], table[k, 2], preferred_element_type=F32)
    source = lax.broadcasted_iota(jnp.int32, (128, 256), 0)
    target = lax.broadcasted_iota(jnp.int32, (128, 256), 1)
    picks[...] = jnp.where(
        ((target < 128) & (source >= 64) & (source < 67)) | ((target >= 128) & (source >= 67) & (source < 70)), 1.0, 0.0
    ).astype(BF16)


    def of_y(target):
        return pl.ds(pl.multiple_of(16 * target, 16), 16)

    routes = ((-4, -2), (-3, -1), (3, 1), (-1, -1), (1, 1))
    for g in range(2):
        for b in range(2):
            i = 2 * g + b
            rows = pl.ds(pl.multiple_of(64 * order[i], 64), 64)
            waits.take(("fwd_recv", i), ("stat_recv", i))
            lookup = stats[rows, :]
            moments = jnp.dot(lookup, picks[...], preferred_element_type=F32)
            for kk in (0, 1):
                mods = jnp.dot(lookup, fields[kk], preferred_element_type=F32)
                for part_of in range(3):
                    at = slice(128 * part_of, 128 * part_of + 128)
                    after = slice(384 + 128 * part_of, 512 + 128 * part_of)
                    goal_at = slice(384 * kk + 128 * part_of, 384 * kk + 128 * part_of + 128)
                    normed[g, 64 * b : 64 * b + 64, goal_at] = (
                        (gathered[kk, rows, at].astype(F32) - moments[:, 0:128])
                        * moments[:, 128:256]
                        * (1.0 + mods[:, after])
                        + mods[:, at]
                    ).astype(BF16)
        if g == 0:
            waits.take(("share_recv", 1), ("share_recv", 2))
        part[g] = jnp.dot(normed[g], w1[...], preferred_element_type=F32).astype(BF16)
        for slot, (goal, via) in enumerate(routes):
            send(part.at[g, of_y(at_y(goal, g))], part_in.at[g, slot], part_send, part_recv.at[g, slot], to_y(at_y(via, g)))
            waits.owe(("part", g, slot), part_in.at[g, slot], part_recv.at[g, slot])
    for g in range(2):
        waits.take(("part", g, 2))
        relay[g, 1] = (part[g, of_y(at_y(2, g)), :].astype(F32) + part_in[g, 2].astype(F32)).astype(BF16)
        send(relay.at[g, 1], part_in.at[g, 6], part_send, part_recv.at[g, 6], to_y(at_y(2, g)))
        waits.take(("part", g, 1), ("part", g, 0))
        relay[g, 0] = (
            part[g, of_y(at_y(-2, g)), :].astype(F32) + part_in[g, 1].astype(F32) + part_in[g, 0].astype(F32)
        ).astype(BF16)
        send(relay.at[g, 0], part_in.at[g, 5], part_send, part_recv.at[g, 5], to_y(at_y(-2, g)))
        waits.owe(("part", g, 5), part_in.at[g, 5], part_recv.at[g, 5])
        waits.owe(("part", g, 6), part_in.at[g, 6], part_recv.at[g, 6])
    waits.owe("part_send", part_in, part_send)
    mine = of_y(y)
    for g in range(2):
        waits.take(("part", g, 3), ("part", g, 4), ("part", g, 6), ("part", g, 5))
        gate_up = part[g, mine, :].astype(F32) + jnp.sum(part_in[g, 3:7].astype(F32), axis=0)
        gate, up = gate_up[:, 0:512], gate_up[:, 512:1024]
        hidden[g, mine, :] = (gate / (1.0 + jnp.exp(-gate)) * up).astype(BF16)
        for dy in far_y[:-1]:
            send(hidden.at[g, mine], hidden.at[g, mine], hid_send, hid_recv.at[g], to_y(around_y[dy]))
        waits.owe(("hidden", g), hidden.at[0, pl.ds(0, 112)], hid_recv.at[g])
    waits.owe("hid_send", hidden.at[:, pl.ds(0, 112)], hid_send)
    waits.take("sum_send", "tok_send", "fwd_send", "stat_send", "share_send", "part_send")
    waits.take(("share_recv", 3))

    for g in range(2):
        waits.take(("hidden", g))
        for kk in (0, 1):
            share = jnp.dot(hidden[g], w2[kk], preferred_element_type=F32).astype(BF16)
            for b in range(2):
                for goal_x in range(NX):
                    at = 64 * b + 16 * goal_x
                    down[2 * g + b, goal_x, kk] = share[at : at + 16, :]
        for i in (2 * g, 2 * g + 1):
            for dx in (2, 1, 3):
                to = around_x[dx]
                send(down.at[i, to], down_in.at[i, dx - 1], dx_send, dx_recv.at[i], to_x(to))
            waits.owe(("down", i), down_in.at[i], dx_recv.at[i])
    waits.owe("dx_send", down_in, dx_send)
    for i in range(4):
        waits.take(("down", i))
        for kk in (0, 1):
            down_mid[i, kk] = (
                down[i, x, kk].astype(F32) + jnp.sum(down_in[i, :, kk].astype(F32), axis=0)
            ).astype(BF16)
        goal = 4 * k + order[i]
        send(down_mid.at[i, 1 - k], branch_in.at[z], dz_send, dz_recv, place(y, 1 - k, goal, x))

        @pl.when(goal == z)
        def _(i=i):
            pltpu.make_async_copy(down_mid.at[i, k], branch_in.at[z], dz_recv).start()

        @pl.when(goal != z)
        def _(i=i, goal=goal):
            send(down_mid.at[i, k], branch_in.at[z], dz_send, dz_recv, place(y, k, goal, x))

    waits.owe("dz_recv", branch_in, dz_recv)
    waits.owe("dz_send", branch_in.at[pl.ds(0, 7)], dz_send)
    waits.owe("dz_send", own, dz_send, k != hz)
    waits.take("hid_send", "dz_recv")
    branch = jnp.sum(branch_in[...].astype(F32), axis=0)
    out[...] = (own[...].astype(F32) + gate_mod * branch).astype(BF16)
    waits.take("dx_send", "dz_send")


def on_device(tokens, token_frame, noise_level, modulation, gate_weight, up_weight, down_weight):
    hbm = pl.BlockSpec(memory_space=pltpu.HBM)
    vmem, dma = pltpu.VMEM, pltpu.SemaphoreType.DMA
    return pl.pallas_call(
        kernel,
        out_shape=jax.ShapeDtypeStruct((16, 384), BF16),
        in_specs=[hbm, hbm, hbm, hbm, hbm, hbm, hbm],
        out_specs=pl.BlockSpec(memory_space=pltpu.VMEM),
        scratch_shapes=[
            vmem((16, 384), BF16),
            vmem((2, 3, 64, 384), BF16),
            vmem((768, 1024), BF16),
            vmem((2, 512, 384), BF16),
            vmem((1, 1, 128), F32),
            vmem((16, 1, 128), F32),
            vmem((16, 128), BF16),
            vmem((256, 128), BF16),
            vmem((2, 256, 384), BF16),
            vmem((2, 128, 768), BF16),
            vmem((128, 256), BF16),
            vmem((2, 128, 768), BF16),
            vmem((2, 128, 1024), BF16),
            vmem((2, 7, 16, 1024), BF16),
            vmem((2, 2, 16, 1024), BF16),
            vmem((2, 128, 512), BF16),
            vmem((4, 4, 2, 16, 384), BF16),
            vmem((4, 3, 2, 16, 384), BF16),
            vmem((4, 2, 16, 384), BF16),
            vmem((8, 16, 384), BF16),
            pltpu.SMEM((2, 16), jnp.int32),
            dma((7,)),
            dma((4,)),
            dma((4,)),
            dma,
            dma,
            dma,
            dma((4, 2)),
            dma,
            dma((4,)),
            dma,
            dma((4,)),
            dma((4,)),
            dma,
            dma((2, 7)),
            dma,
            dma((2,)),
            dma,
            dma((4,)),
            dma,
            dma,
            pltpu.SemaphoreType.REGULAR((2,)),
        ],
        compiler_params=pltpu.CompilerParams(
            collective_id=0, has_side_effects=True, vmem_limit_bytes=60 << 20
        ),
        cost_estimate=pl.CostEstimate(flops=604_000_000, bytes_accessed=1_400_000, transcendentals=16384),
        name="modulated_feed_forward",
    )(tokens, token_frame, noise_level, jnp.transpose(modulation, (1, 0, 2)), gate_weight, up_weight, down_weight)


def solution(mesh):
    placed = (
        P("col", "row"),
        P("col"),
        P(),
        P(None, None, "row"),
        P("row", "col"),
        P("row", "col"),
        P("col", "row"),
    )
    return jax.shard_map(
        on_device, mesh=mesh, in_specs=placed, out_specs=P("col", "row"), check_vma=False
    )
```

```python
import functools

import jax
import jax.numpy as jnp
from jax import lax
from jax.experimental import pallas as pl
from jax.experimental.pallas import tpu as pltpu
from jax.sharding import PartitionSpec as P

D = 6144
EPS = 1e-06
NY, NZ, NX = 8, 8, 4
MESH = pl.DeviceIdType.MESH
F32, BF16 = jnp.float32, jnp.bfloat16


def place(y, core, z, x):
    return (y * 2 + core, z * NX + x)


def pieces(value):
    high = value.astype(BF16).astype(F32)
    rest = value - high
    middle = rest.astype(BF16).astype(F32)
    return high, middle, rest - middle


def in_lanes(lane, first, columns, base):
    for i, column in enumerate(columns):
        base = jnp.where(lane == first + i, column, base)
    return base


def send(src, dst, send_sem, recv_sem, device):
    pltpu.make_async_remote_copy(
        src, dst, send_sem, recv_sem, device_id=device, device_id_type=MESH
    ).start()


def await_bytes(ref, sem):
    pltpu.make_async_copy(ref, ref, sem).wait()


class Waits:
    def __init__(self):
        self.owed = {}

    def owe(self, name, ref, sem, when=None):
        self.owed.setdefault(name, []).append((ref, sem, when))

    def take(self, *names):
        for name in names:
            for ref, sem, when in self.owed.pop(name):
                if when is None:
                    await_bytes(ref, sem)
                else:
                    pl.when(when)(lambda ref=ref, sem=sem: await_bytes(ref, sem))


def kernel(
    tokens, frame, noise, modulation, gate_w, up_w, down_w, out,
    own, table, w1, w2, sum_out, sum_in, stat_out, stats, gathered, fields, picks,
    normed, part, part_in, relay, hidden, down, down_in, down_mid, branch_in, levels,
    local_sem, share_send, share_recv, sum_send, sum_recv, tok_send, tok_recv,
    fwd_send, fwd_recv, stat_send, stat_recv, statf_recv, part_send, part_recv, hid_send, hid_recv,
    dx_send, dx_recv, dz_send, dz_recv, ready,
):
    row, col = lax.axis_index("row"), lax.axis_index("col")
    y, k, z, x = row // 2, row % 2, col // NX, col % NX
    hz = z // 4
    zz = z % 4
    way = 1 - 2 * k
    sibling = place(y, 1 - k, z, x)
    waits = Waits()

    def at_y(step, chunk):
        return lax.rem(y + 8 + (step if chunk == 0 else -step) * way, NY)

    def to_y(target):
        return place(target, k, z, x)

    def to_x(target):
        return place(y, k, z, target)

    upper = zz // 2
    outward = [zz, 1 - zz + 4 * upper, 2 - upper, 3 - 3 * upper]
    holds = 1 - (k - hz) * (k - hz)
    near_first = [outward[i] * holds + outward[3 - i] * (1 - holds) for i in range(4)]
    order = [i * (1 - k) + near_first[i] * k for i in range(4)]
    around_z = {dz: lax.rem(z + dz, NZ) for dz in range(1, NZ)}
    around_y = {dy: lax.rem(y + dy, NY) for dy in range(NY)}
    around_x = {dx: lax.rem(x + dx, NX) for dx in range(1, NX)}
    far_z, far_y = (4, 3, 5, 2, 6, 1, 7), (4, 3, 5, 2, 6, 1, 7, 0)

    own_copy = pltpu.make_async_copy(tokens, own, local_sem.at[0])
    own_copy.start()
    small = [
        pltpu.make_async_copy(frame, levels.at[0], local_sem.at[5]),
        pltpu.make_async_copy(noise, levels.at[1], local_sem.at[6]),
    ]
    for copy in small:
        copy.start()
    barrier = pltpu.get_barrier_semaphore()

    def enter(device):
        pl.semaphore_signal(barrier, inc=1, device_id=device, device_id_type=MESH)

    for dz in far_z:
        enter(place(y, 1, around_z[dz], x))
    @pl.when(k == 1)
    def _():
        for from_z in range(4, NZ):

            @pl.when(from_z != z)
            def _(from_z=from_z):
                for dx in (2, 1, 3):
                    enter(place(y, 1, from_z, around_x[dx]))

    for dy in far_y[:-1]:
        enter(place(around_y[dy], 0, z, x))
    for dx in (2, 1, 3):
        enter(place(y, 0, z, around_x[dx]))
    enter(sibling)

    own_copy.wait()
    wide = own[...].astype(F32)
    lane = lax.broadcasted_iota(jnp.int32, (16, 128), 1)
    sublane = lax.broadcasted_iota(jnp.int32, (16, 128), 0)
    zero = jnp.zeros((16, 128), F32)
    square = jnp.sum(wide * wide, axis=1, keepdims=True)
    spread_out = jnp.where(lane == sublane, jnp.sum(wide, axis=1, keepdims=True), zero)
    spread_out = jnp.where(lane == sublane + 16, square, spread_out)
    sums = jnp.sum(spread_out, axis=0, keepdims=True)
    sum_out[0] = sums
    sum_in[row] = sums

    @pl.when(k == 0)
    def _():
        pl.semaphore_wait(barrier, 21)
        pl.semaphore_signal(ready.at[0], inc=1, device_id=sibling, device_id_type=MESH)

    @pl.when(k == 1)
    def _():
        pl.semaphore_wait(ready.at[0], 1)

    for dy in far_y:
        for core in (k, 1 - k) if dy else (1 - k,):
            send(sum_out.at[0], sum_in.at[row], sum_send, sum_recv, place(around_y[dy], core, z, x))
    waits.owe("sum_send", sum_in.at[pl.ds(0, 15)], sum_send)
    waits.owe("sum_recv", sum_in.at[pl.ds(0, 15)], sum_recv)

    half = w1.at[pl.ds(0, 384), pl.ds(0, 512)]
    rows = pl.ds(384 * k, 384)
    shared = (
        (modulation, table.at[k], table.at[0]),
        (gate_w, w1.at[rows, pl.ds(0, 512)], half),
        (up_w, w1.at[rows, pl.ds(512, 512)], half),
        (down_w, w2.at[k], w2.at[0]),
    )
    for i, (_, _, like) in enumerate(shared):
        waits.owe("share_send", like, share_send.at[i])
        waits.owe(("share_recv", i), like, share_recv.at[i])
        waits.owe(("share_recv", i), like, local_sem.at[1 + i])

    def share():
        for i, (source, goal, _) in enumerate(shared):
            pltpu.make_async_copy(source, goal, local_sem.at[1 + i]).start()
            send(source, goal, share_send.at[i], share_recv.at[i], sibling)

    pl.when(hz == 0)(share)

    @pl.when(k == 1)
    def _():
        pl.semaphore_wait(barrier, 15 + 21 * hz)
        pl.semaphore_signal(ready.at[1], inc=1, device_id=sibling, device_id_type=MESH)

    @pl.when(k == 0)
    def _():
        pl.semaphore_wait(ready.at[1], 1)

    block = pl.ds(64 * zz + 16 * x, 16)
    for to_z in [4 * (1 - hz) + lax.rem(zz + d, 4) for d in (0, 1, 3, 2)] + [4 * hz + lax.rem(zz + d, 4) for d in (2, 1, 3)]:
        send(own, gathered.at[k, block], tok_send, tok_recv.at[zz, k], place(y, hz, to_z, x))

    @pl.when(k == hz)
    def _():
        pltpu.make_async_copy(own, gathered.at[k, block], tok_recv.at[zz, k]).start()

    @pl.when(k != hz)
    def _():
        send(own, gathered.at[k, block], tok_send, tok_recv.at[zz, k], sibling)

    waits.owe("tok_send", gathered.at[0, pl.ds(0, 112)], tok_send)
    waits.owe("tok_send", own, tok_send, k != hz)

    pl.when(hz == 1)(share)
    for copy in small:
        copy.wait()
    onehot = zero
    for t in range(16):
        level = levels[1, levels[0, t]]
        onehot = jnp.where((sublane == t) & (lane == level), 1.0, onehot)

    waits.take("sum_recv")
    total = jnp.broadcast_to(jnp.sum(sum_in[:, 0, :], axis=0, keepdims=True), (16, 128))
    center = jnp.sum(jnp.where(lane == sublane, total, zero), axis=1, keepdims=True) / D
    square = jnp.sum(jnp.where(lane == sublane + 16, total, zero), axis=1, keepdims=True) / D
    scale = lax.rsqrt(square - center * center + EPS)
    stat_out[...] = in_lanes(lane, 64, pieces(center) + pieces(scale), onehot).astype(BF16)

    @pl.when((k == 1) & (hz == 1))
    def _():
        for dz in far_z:
            for to in (around_x[2], around_x[1], around_x[3], x):
                send(stat_out, stats.at[block], stat_send, stat_recv.at[zz], place(y, k, around_z[dz], to))
        for dx in (2, 1, 3):
            send(stat_out, stats.at[block], stat_send, stat_recv.at[zz], to_x(around_x[dx]))
        pltpu.make_async_copy(stat_out, stats.at[block], stat_recv.at[zz]).start()

    @pl.when((k == 0) & (hz == 0))
    def _():
        for dz in far_z:
            send(stat_out, stats.at[block], stat_send, stat_recv.at[zz], place(y, k, around_z[dz], x))
        pltpu.make_async_copy(stat_out, stats.at[block], stat_recv.at[zz]).start()

    waits.owe("stat_send", stats, stat_send, (k == 1) & (hz == 1))
    waits.owe("stat_send", stats.at[pl.ds(0, 240)], stat_send, (k == 1) & (hz == 1))
    waits.owe("stat_send", stats.at[pl.ds(0, 112)], stat_send, (k == 0) & (hz == 0))
    waits.owe("stat_send", stats.at[pl.ds(0, 192)], stat_send, k == 0)

    def forward(like, from_z, send_sem, recv_sem):
        for dx in (2, 1, 3):
            send(like, like, send_sem, recv_sem.at[from_z], to_x(around_x[dx]))

    def forward_stats(from_z):
        came = stats.at[pl.ds(64 * from_z + 16 * x, 16)]
        await_bytes(came, stat_recv.at[from_z])
        forward(came, from_z, stat_send, statf_recv)

    for i, from_z in enumerate(order):
        for kk in (0, 1):
            came = gathered.at[kk, pl.ds(64 * from_z + 16 * x, 16)]
            await_bytes(came, tok_recv.at[from_z, kk])
            forward(came, from_z, fwd_send, fwd_recv)
        if i % 2:
            for near in order[i - 1 : i + 1]:
                pl.when(k == 0)(functools.partial(forward_stats, near))
    for i in range(4):
        waits.owe(("stat_recv", i), stats.at[pl.ds(0, 48)], statf_recv.at[order[i]], k == 0)
        waits.owe(("stat_recv", i), stats.at[pl.ds(0, 64)], stat_recv.at[order[i]], k == 1)
    waits.owe("fwd_send", gathered.at[:, pl.ds(0, 192)], fwd_send)
    for i in range(4):
        waits.owe(("fwd_recv", i), gathered.at[:, pl.ds(0, 48)], fwd_recv.at[order[i]])

    waits.take(("share_recv", 0))
    for kk in (0, 1):
        fields[kk, 64:128, :] = jnp.zeros((64, 768), BF16)
        fields[kk, 0:64, 0:384] = table[kk, 0]
        fields[kk, 0:64, 384:768] = table[kk, 1]
    gate_mod = jnp.dot(onehot.astype(BF16)[:, 0:64], table[k, 2], preferred_element_type=F32)
    source = lax.broadcasted_iota(jnp.int32, (128, 256), 0)
    target = lax.broadcasted_iota(jnp.int32, (128, 256), 1)
    picks[...] = jnp.where(
        ((target < 128) & (source >= 64) & (source < 67)) | ((target >= 128) & (source >= 67) & (source < 70)), 1.0, 0.0
    ).astype(BF16)


    def of_y(target):
        return pl.ds(pl.multiple_of(16 * target, 16), 16)

    routes = ((-4, -2), (-3, -1), (3, 1), (-1, -1), (1, 1))
    for g in range(2):
        for b in range(2):
            i = 2 * g + b
            rows = pl.ds(pl.multiple_of(64 * order[i], 64), 64)
            waits.take(("fwd_recv", i), ("stat_recv", i))
            lookup = stats[rows, :]
            moments = jnp.dot(lookup, picks[...], preferred_element_type=F32)
            for kk in (0, 1):
                mods = jnp.dot(lookup, fields[kk], preferred_element_type=F32)
                for part_of in range(3):
                    at = slice(128 * part_of, 128 * part_of + 128)
                    after = slice(384 + 128 * part_of, 512 + 128 * part_of)
                    goal_at = slice(384 * kk + 128 * part_of, 384 * kk + 128 * part_of + 128)
                    normed[g, 64 * b : 64 * b + 64, goal_at] = (
                        (gathered[kk, rows, at].astype(F32) - moments[:, 0:128])
                        * moments[:, 128:256]
                        * (1.0 + mods[:, after])
                        + mods[:, at]
                    ).astype(BF16)
        if g == 0:
            waits.take(("share_recv", 1), ("share_recv", 2))
        part[g] = jnp.dot(normed[g], w1[...], preferred_element_type=F32).astype(BF16)
        for slot, (goal, via) in enumerate(routes):
            send(part.at[g, of_y(at_y(goal, g))], part_in.at[g, slot], part_send, part_recv.at[g, slot], to_y(at_y(via, g)))
            waits.owe(("part", g, slot), part_in.at[g, slot], part_recv.at[g, slot])
    for g in range(2):
        waits.take(("part", g, 2))
        relay[g, 1] = (part[g, of_y(at_y(2, g)), :].astype(F32) + part_in[g, 2].astype(F32)).astype(BF16)
        send(relay.at[g, 1], part_in.at[g, 6], part_send, part_recv.at[g, 6], to_y(at_y(2, g)))
        waits.take(("part", g, 1), ("part", g, 0))
        relay[g, 0] = (
            part[g, of_y(at_y(-2, g)), :].astype(F32) + part_in[g, 1].astype(F32) + part_in[g, 0].astype(F32)
        ).astype(BF16)
        send(relay.at[g, 0], part_in.at[g, 5], part_send, part_recv.at[g, 5], to_y(at_y(-2, g)))
        waits.owe(("part", g, 5), part_in.at[g, 5], part_recv.at[g, 5])
        waits.owe(("part", g, 6), part_in.at[g, 6], part_recv.at[g, 6])
    waits.owe("part_send", part_in, part_send)
    mine = of_y(y)
    for g in range(2):
        waits.take(("part", g, 3), ("part", g, 4), ("part", g, 6), ("part", g, 5))
        gate_up = part[g, mine, :].astype(F32) + jnp.sum(part_in[g, 3:7].astype(F32), axis=0)
        gate, up = gate_up[:, 0:512], gate_up[:, 512:1024]
        hidden[g, mine, :] = (gate / (1.0 + jnp.exp(-gate)) * up).astype(BF16)
        for dy in far_y[:-1]:
            send(hidden.at[g, mine], hidden.at[g, mine], hid_send, hid_recv.at[g], to_y(around_y[dy]))
        waits.owe(("hidden", g), hidden.at[0, pl.ds(0, 112)], hid_recv.at[g])
    waits.owe("hid_send", hidden.at[:, pl.ds(0, 112)], hid_send)
    waits.take("sum_send", "tok_send", "fwd_send", "stat_send", "share_send", "part_send")
    waits.take(("share_recv", 3))

    for g in range(2):
        waits.take(("hidden", g))
        for kk in (0, 1):
            share = jnp.dot(hidden[g], w2[kk], preferred_element_type=F32).astype(BF16)
            for b in range(2):
                for goal_x in range(NX):
                    at = 64 * b + 16 * goal_x
                    down[2 * g + b, goal_x, kk] = share[at : at + 16, :]
        for i in (2 * g, 2 * g + 1):
            for dx in (2, 1, 3):
                to = around_x[dx]
                send(down.at[i, to], down_in.at[i, dx - 1], dx_send, dx_recv.at[i], to_x(to))
            waits.owe(("down", i), down_in.at[i], dx_recv.at[i])
    waits.owe("dx_send", down_in, dx_send)
    for i in range(4):
        waits.take(("down", i))
        for kk in (0, 1):
            down_mid[i, kk] = (
                down[i, x, kk].astype(F32) + jnp.sum(down_in[i, :, kk].astype(F32), axis=0)
            ).astype(BF16)
        goal = 4 * k + order[i]
        send(down_mid.at[i, 1 - k], branch_in.at[z], dz_send, dz_recv, place(y, 1 - k, goal, x))

        @pl.when(goal == z)
        def _(i=i):
            pltpu.make_async_copy(down_mid.at[i, k], branch_in.at[z], dz_recv).start()

        @pl.when(goal != z)
        def _(i=i, goal=goal):
            send(down_mid.at[i, k], branch_in.at[z], dz_send, dz_recv, place(y, k, goal, x))

    waits.owe("dz_recv", branch_in, dz_recv)
    waits.owe("dz_send", branch_in.at[pl.ds(0, 7)], dz_send)
    waits.owe("dz_send", own, dz_send, k != hz)
    waits.take("hid_send", "dz_recv")
    branch = jnp.sum(branch_in[...].astype(F32), axis=0)
    out[...] = (own[...].astype(F32) + gate_mod * branch).astype(BF16)
    waits.take("dx_send", "dz_send")


def on_device(tokens, token_frame, noise_level, modulation, gate_weight, up_weight, down_weight):
    hbm = pl.BlockSpec(memory_space=pltpu.HBM)
    vmem, dma = pltpu.VMEM, pltpu.SemaphoreType.DMA
    return pl.pallas_call(
        kernel,
        out_shape=jax.ShapeDtypeStruct((16, 384), BF16),
        in_specs=[hbm, hbm, hbm, hbm, hbm, hbm, hbm],
        out_specs=pl.BlockSpec(memory_space=pltpu.VMEM),
        scratch_shapes=[
            vmem((16, 384), BF16),
            vmem((2, 3, 64, 384), BF16),
            vmem((768, 1024), BF16),
            vmem((2, 512, 384), BF16),
            vmem((1, 1, 128), F32),
            vmem((16, 1, 128), F32),
            vmem((16, 128), BF16),
            vmem((256, 128), BF16),
            vmem((2, 256, 384), BF16),
            vmem((2, 128, 768), BF16),
            vmem((128, 256), BF16),
            vmem((2, 128, 768), BF16),
            vmem((2, 128, 1024), BF16),
            vmem((2, 7, 16, 1024), BF16),
            vmem((2, 2, 16, 1024), BF16),
            vmem((2, 128, 512), BF16),
            vmem((4, 4, 2, 16, 384), BF16),
            vmem((4, 3, 2, 16, 384), BF16),
            vmem((4, 2, 16, 384), BF16),
            vmem((8, 16, 384), BF16),
            pltpu.SMEM((2, 16), jnp.int32),
            dma((7,)),
            dma((4,)),
            dma((4,)),
            dma,
            dma,
            dma,
            dma((4, 2)),
            dma,
            dma((4,)),
            dma,
            dma((4,)),
            dma((4,)),
            dma,
            dma((2, 7)),
            dma,
            dma((2,)),
            dma,
            dma((4,)),
            dma,
            dma,
            pltpu.SemaphoreType.REGULAR((2,)),
        ],
        compiler_params=pltpu.CompilerParams(
            collective_id=0, has_side_effects=True, vmem_limit_bytes=60 << 20
        ),
        cost_estimate=pl.CostEstimate(flops=604_000_000, bytes_accessed=1_400_000, transcendentals=16384),
        name="modulated_feed_forward",
    )(tokens, token_frame, noise_level, jnp.transpose(modulation, (1, 0, 2)), gate_weight, up_weight, down_weight)


def solution(mesh):
    placed = (
        P("col", "row"),
        P("col"),
        P(),
        P(None, None, "row"),
        P("row", "col"),
        P("row", "col"),
        P("col", "row"),
    )
    return jax.shard_map(
        on_device, mesh=mesh, in_specs=placed, out_specs=P("col", "row"), check_vma=False
    )
```

```python
import functools

import jax
import jax.numpy as jnp
from jax import lax
from jax.experimental import pallas as pl
from jax.experimental.pallas import tpu as pltpu
from jax.sharding import PartitionSpec as P

D = 6144
EPS = 1e-06
NY, NZ, NX = 8, 8, 4
MESH = pl.DeviceIdType.MESH
F32, BF16 = jnp.float32, jnp.bfloat16


def place(y, core, z, x):
    return (y * 2 + core, z * NX + x)


def pieces(value):
    high = value.astype(BF16).astype(F32)
    rest = value - high
    middle = rest.astype(BF16).astype(F32)
    return high, middle, rest - middle


def in_lanes(lane, first, columns, base):
    for i, column in enumerate(columns):
        base = jnp.where(lane == first + i, column, base)
    return base


def send(src, dst, send_sem, recv_sem, device):
    pltpu.make_async_remote_copy(
        src, dst, send_sem, recv_sem, device_id=device, device_id_type=MESH
    ).start()


def await_bytes(ref, sem):
    pltpu.make_async_copy(ref, ref, sem).wait()


class Waits:
    def __init__(self):
        self.owed = {}

    def owe(self, name, ref, sem, when=None):
        self.owed.setdefault(name, []).append((ref, sem, when))

    def take(self, *names):
        for name in names:
            for ref, sem, when in self.owed.pop(name):
                if when is None:
                    await_bytes(ref, sem)
                else:
                    pl.when(when)(lambda ref=ref, sem=sem: await_bytes(ref, sem))


def kernel(
    tokens, frame, noise, modulation, gate_w, up_w, down_w, out,
    own, table, w1, w2, sum_out, sum_in, stat_out, stats, gathered, fields, picks,
    normed, part, part_in, relay, hidden, down, down_in, down_mid, branch_in, levels,
    local_sem, share_send, share_recv, sum_send, sum_recv, tok_send, tok_recv,
    fwd_send, fwd_recv, stat_send, stat_recv, statf_recv, part_send, part_recv, hid_send, hid_recv,
    dx_send, dx_recv, dz_send, dz_recv, ready,
):
    row, col = lax.axis_index("row"), lax.axis_index("col")
    y, k, z, x = row // 2, row % 2, col // NX, col % NX
    hz = z // 4
    zz = z % 4
    way = 1 - 2 * k
    sibling = place(y, 1 - k, z, x)
    waits = Waits()

    def at_y(step, chunk):
        return lax.rem(y + 8 + (step if chunk == 0 else -step) * way, NY)

    def to_y(target):
        return place(target, k, z, x)

    def to_x(target):
        return place(y, k, z, target)

    upper = zz // 2
    outward = [zz, 1 - zz + 4 * upper, 2 - upper, 3 - 3 * upper]
    holds = 1 - (k - hz) * (k - hz)
    near_first = [outward[i] * holds + outward[3 - i] * (1 - holds) for i in range(4)]
    order = [i * (1 - k) + (3 - i) * k for i in range(4)]
    around_z = {dz: lax.rem(z + dz, NZ) for dz in range(1, NZ)}
    around_y = {dy: lax.rem(y + dy, NY) for dy in range(NY)}
    around_x = {dx: lax.rem(x + dx, NX) for dx in range(1, NX)}
    far_z, far_y = (4, 3, 5, 2, 6, 1, 7), (4, 3, 5, 2, 6, 1, 7, 0)

    own_copy = pltpu.make_async_copy(tokens, own, local_sem.at[0])
    own_copy.start()
    small = [
        pltpu.make_async_copy(frame, levels.at[0], local_sem.at[5]),
        pltpu.make_async_copy(noise, levels.at[1], local_sem.at[6]),
    ]
    for copy in small:
        copy.start()
    barrier = pltpu.get_barrier_semaphore()

    def enter(device):
        pl.semaphore_signal(barrier, inc=1, device_id=device, device_id_type=MESH)

    for dz in far_z:
        enter(place(y, 1, around_z[dz], x))
    @pl.when(k == 1)
    def _():
        for from_z in range(4, NZ):

            @pl.when(from_z != z)
            def _(from_z=from_z):
                for dx in (2, 1, 3):
                    enter(place(y, 1, from_z, around_x[dx]))

    for dy in far_y[:-1]:
        enter(place(around_y[dy], 0, z, x))
    for dx in (2, 1, 3):
        enter(place(y, 0, z, around_x[dx]))
    enter(sibling)

    own_copy.wait()
    wide = own[...].astype(F32)
    lane = lax.broadcasted_iota(jnp.int32, (16, 128), 1)
    sublane = lax.broadcasted_iota(jnp.int32, (16, 128), 0)
    zero = jnp.zeros((16, 128), F32)
    square = jnp.sum(wide * wide, axis=1, keepdims=True)
    spread_out = jnp.where(lane == sublane, jnp.sum(wide, axis=1, keepdims=True), zero)
    spread_out = jnp.where(lane == sublane + 16, square, spread_out)
    sums = jnp.sum(spread_out, axis=0, keepdims=True)
    sum_out[0] = sums
    sum_in[row] = sums

    @pl.when(k == 0)
    def _():
        pl.semaphore_wait(barrier, 21)
        pl.semaphore_signal(ready.at[0], inc=1, device_id=sibling, device_id_type=MESH)

    @pl.when(k == 1)
    def _():
        pl.semaphore_wait(ready.at[0], 1)

    for dy in far_y:
        for core in (k, 1 - k) if dy else (1 - k,):
            send(sum_out.at[0], sum_in.at[row], sum_send, sum_recv, place(around_y[dy], core, z, x))
    waits.owe("sum_send", sum_in.at[pl.ds(0, 15)], sum_send)
    waits.owe("sum_recv", sum_in.at[pl.ds(0, 15)], sum_recv)

    half = w1.at[pl.ds(0, 384), pl.ds(0, 512)]
    rows = pl.ds(384 * k, 384)
    shared = (
        (modulation, table.at[k], table.at[0]),
        (gate_w, w1.at[rows, pl.ds(0, 512)], half),
        (up_w, w1.at[rows, pl.ds(512, 512)], half),
        (down_w, w2.at[k], w2.at[0]),
    )
    for i, (_, _, like) in enumerate(shared):
        waits.owe("share_send", like, share_send.at[i])
        waits.owe(("share_recv", i), like, share_recv.at[i])
        waits.owe(("share_recv", i), like, local_sem.at[1 + i])

    def share():
        for i, (source, goal, _) in enumerate(shared):
            pltpu.make_async_copy(source, goal, local_sem.at[1 + i]).start()
            send(source, goal, share_send.at[i], share_recv.at[i], sibling)

    pl.when(hz == 0)(share)

    @pl.when(k == 1)
    def _():
        pl.semaphore_wait(barrier, 15 + 21 * hz)
        pl.semaphore_signal(ready.at[1], inc=1, device_id=sibling, device_id_type=MESH)

    @pl.when(k == 0)
    def _():
        pl.semaphore_wait(ready.at[1], 1)

    block = pl.ds(64 * zz + 16 * x, 16)
    for to_z in [4 * (1 - hz) + lax.rem(zz + d, 4) for d in (0, 1, 3, 2)] + [4 * hz + lax.rem(zz + d, 4) for d in (2, 1, 3)]:
        send(own, gathered.at[k, block], tok_send, tok_recv.at[zz, k], place(y, hz, to_z, x))

    @pl.when(k == hz)
    def _():
        pltpu.make_async_copy(own, gathered.at[k, block], tok_recv.at[zz, k]).start()

    @pl.when(k != hz)
    def _():
        send(own, gathered.at[k, block], tok_send, tok_recv.at[zz, k], sibling)

    waits.owe("tok_send", gathered.at[0, pl.ds(0, 112)], tok_send)
    waits.owe("tok_send", own, tok_send, k != hz)

    pl.when(hz == 1)(share)
    for copy in small:
        copy.wait()
    onehot = zero
    for t in range(16):
        level = levels[1, levels[0, t]]
        onehot = jnp.where((sublane == t) & (lane == level), 1.0, onehot)

    waits.take("sum_recv")
    total = jnp.broadcast_to(jnp.sum(sum_in[:, 0, :], axis=0, keepdims=True), (16, 128))
    center = jnp.sum(jnp.where(lane == sublane, total, zero), axis=1, keepdims=True) / D
    square = jnp.sum(jnp.where(lane == sublane + 16, total, zero), axis=1, keepdims=True) / D
    scale = lax.rsqrt(square - center * center + EPS)
    stat_out[...] = in_lanes(lane, 64, pieces(center) + pieces(scale), onehot).astype(BF16)

    @pl.when((k == 1) & (hz == 1))
    def _():
        for dz in far_z:
            for to in (around_x[2], around_x[1], around_x[3], x):
                send(stat_out, stats.at[block], stat_send, stat_recv.at[zz], place(y, k, around_z[dz], to))
        for dx in (2, 1, 3):
            send(stat_out, stats.at[block], stat_send, stat_recv.at[zz], to_x(around_x[dx]))
        pltpu.make_async_copy(stat_out, stats.at[block], stat_recv.at[zz]).start()

    @pl.when((k == 0) & (hz == 0))
    def _():
        for dz in far_z:
            send(stat_out, stats.at[block], stat_send, stat_recv.at[zz], place(y, k, around_z[dz], x))
        pltpu.make_async_copy(stat_out, stats.at[block], stat_recv.at[zz]).start()

    waits.owe("stat_send", stats, stat_send, (k == 1) & (hz == 1))
    waits.owe("stat_send", stats.at[pl.ds(0, 240)], stat_send, (k == 1) & (hz == 1))
    waits.owe("stat_send", stats.at[pl.ds(0, 112)], stat_send, (k == 0) & (hz == 0))
    waits.owe("stat_send", stats.at[pl.ds(0, 192)], stat_send, k == 0)

    def forward(like, from_z, send_sem, recv_sem):
        for dx in (2, 1, 3):
            send(like, like, send_sem, recv_sem.at[from_z], to_x(around_x[dx]))

    def forward_stats(from_z):
        came = stats.at[pl.ds(64 * from_z + 16 * x, 16)]
        await_bytes(came, stat_recv.at[from_z])
        forward(came, from_z, stat_send, statf_recv)

    for i, from_z in enumerate(order):
        for kk in (0, 1):
            came = gathered.at[kk, pl.ds(64 * from_z + 16 * x, 16)]
            await_bytes(came, tok_recv.at[from_z, kk])
            forward(came, from_z, fwd_send, fwd_recv)
        if i % 2:
            for near in order[i - 1 : i + 1]:
                pl.when(k == 0)(functools.partial(forward_stats, near))
    for i in range(4):
        waits.owe(("stat_recv", i), stats.at[pl.ds(0, 48)], statf_recv.at[order[i]], k == 0)
        waits.owe(("stat_recv", i), stats.at[pl.ds(0, 64)], stat_recv.at[order[i]], k == 1)
    waits.owe("fwd_send", gathered.at[:, pl.ds(0, 192)], fwd_send)
    for i in range(4):
        waits.owe(("fwd_recv", i), gathered.at[:, pl.ds(0, 48)], fwd_recv.at[order[i]])

    waits.take(("share_recv", 0))
    for kk in (0, 1):
        fields[kk, 64:128, :] = jnp.zeros((64, 768), BF16)
        fields[kk, 0:64, 0:384] = table[kk, 0]
        fields[kk, 0:64, 384:768] = table[kk, 1]
    gate_mod = jnp.dot(onehot.astype(BF16)[:, 0:64], table[k, 2], preferred_element_type=F32)
    source = lax.broadcasted_iota(jnp.int32, (128, 256), 0)
    target = lax.broadcasted_iota(jnp.int32, (128, 256), 1)
    picks[...] = jnp.where(
        ((target < 128) & (source >= 64) & (source < 67)) | ((target >= 128) & (source >= 67) & (source < 70)), 1.0, 0.0
    ).astype(BF16)


    def of_y(target):
        return pl.ds(pl.multiple_of(16 * target, 16), 16)

    routes = ((-4, -2), (-3, -1), (3, 1), (-1, -1), (1, 1))
    for g in range(2):
        for b in range(2):
            i = 2 * g + b
            rows = pl.ds(pl.multiple_of(64 * order[i], 64), 64)
            waits.take(("fwd_recv", i), ("stat_recv", i))
            lookup = stats[rows, :]
            moments = jnp.dot(lookup, picks[...], preferred_element_type=F32)
            for kk in (0, 1):
                mods = jnp.dot(lookup, fields[kk], preferred_element_type=F32)
                for part_of in range(3):
                    at = slice(128 * part_of, 128 * part_of + 128)
                    after = slice(384 + 128 * part_of, 512 + 128 * part_of)
                    goal_at = slice(384 * kk + 128 * part_of, 384 * kk + 128 * part_of + 128)
                    normed[g, 64 * b : 64 * b + 64, goal_at] = (
                        (gathered[kk, rows, at].astype(F32) - moments[:, 0:128])
                        * moments[:, 128:256]
                        * (1.0 + mods[:, after])
                        + mods[:, at]
                    ).astype(BF16)
        if g == 0:
            waits.take(("share_recv", 1), ("share_recv", 2))
        part[g] = jnp.dot(normed[g], w1[...], preferred_element_type=F32).astype(BF16)
        for slot, (goal, via) in enumerate(routes):
            send(part.at[g, of_y(at_y(goal, g))], part_in.at[g, slot], part_send, part_recv.at[g, slot], to_y(at_y(via, g)))
            waits.owe(("part", g, slot), part_in.at[g, slot], part_recv.at[g, slot])
    for g in range(2):
        waits.take(("part", g, 2))
        relay[g, 1] = (part[g, of_y(at_y(2, g)), :].astype(F32) + part_in[g, 2].astype(F32)).astype(BF16)
        send(relay.at[g, 1], part_in.at[g, 6], part_send, part_recv.at[g, 6], to_y(at_y(2, g)))
        waits.take(("part", g, 1), ("part", g, 0))
        relay[g, 0] = (
            part[g, of_y(at_y(-2, g)), :].astype(F32) + part_in[g, 1].astype(F32) + part_in[g, 0].astype(F32)
        ).astype(BF16)
        send(relay.at[g, 0], part_in.at[g, 5], part_send, part_recv.at[g, 5], to_y(at_y(-2, g)))
        waits.owe(("part", g, 5), part_in.at[g, 5], part_recv.at[g, 5])
        waits.owe(("part", g, 6), part_in.at[g, 6], part_recv.at[g, 6])
    waits.owe("part_send", part_in, part_send)
    mine = of_y(y)
    for g in range(2):
        waits.take(("part", g, 3), ("part", g, 4), ("part", g, 6), ("part", g, 5))
        gate_up = part[g, mine, :].astype(F32) + jnp.sum(part_in[g, 3:7].astype(F32), axis=0)
        gate, up = gate_up[:, 0:512], gate_up[:, 512:1024]
        hidden[g, mine, :] = (gate / (1.0 + jnp.exp(-gate)) * up).astype(BF16)
        for dy in far_y[:-1]:
            send(hidden.at[g, mine], hidden.at[g, mine], hid_send, hid_recv.at[g], to_y(around_y[dy]))
        waits.owe(("hidden", g), hidden.at[0, pl.ds(0, 112)], hid_recv.at[g])
    waits.owe("hid_send", hidden.at[:, pl.ds(0, 112)], hid_send)
    waits.take("sum_send", "tok_send", "fwd_send", "stat_send", "share_send", "part_send")
    waits.take(("share_recv", 3))

    for g in range(2):
        waits.take(("hidden", g))
        for kk in (0, 1):
            share = jnp.dot(hidden[g], w2[kk], preferred_element_type=F32).astype(BF16)
            for b in range(2):
                for goal_x in range(NX):
                    at = 64 * b + 16 * goal_x
                    down[2 * g + b, goal_x, kk] = share[at : at + 16, :]
        for i in (2 * g, 2 * g + 1):
            for dx in (2, 1, 3):
                to = around_x[dx]
                send(down.at[i, to], down_in.at[i, dx - 1], dx_send, dx_recv.at[i], to_x(to))
            waits.owe(("down", i), down_in.at[i], dx_recv.at[i])
    waits.owe("dx_send", down_in, dx_send)
    for i in range(4):
        waits.take(("down", i))
        for kk in (0, 1):
            down_mid[i, kk] = (
                down[i, x, kk].astype(F32) + jnp.sum(down_in[i, :, kk].astype(F32), axis=0)
            ).astype(BF16)
        goal = 4 * k + order[i]
        send(down_mid.at[i, 1 - k], branch_in.at[z], dz_send, dz_recv, place(y, 1 - k, goal, x))

        @pl.when(goal == z)
        def _(i=i):
            pltpu.make_async_copy(down_mid.at[i, k], branch_in.at[z], dz_recv).start()

        @pl.when(goal != z)
        def _(i=i, goal=goal):
            send(down_mid.at[i, k], branch_in.at[z], dz_send, dz_recv, place(y, k, goal, x))

    waits.owe("dz_recv", branch_in, dz_recv)
    waits.owe("dz_send", branch_in.at[pl.ds(0, 7)], dz_send)
    waits.owe("dz_send", own, dz_send, k != hz)
    waits.take("hid_send", "dz_recv")
    branch = jnp.sum(branch_in[...].astype(F32), axis=0)
    out[...] = (own[...].astype(F32) + gate_mod * branch).astype(BF16)
    waits.take("dx_send", "dz_send")


def on_device(tokens, token_frame, noise_level, modulation, gate_weight, up_weight, down_weight):
    hbm = pl.BlockSpec(memory_space=pltpu.HBM)
    vmem, dma = pltpu.VMEM, pltpu.SemaphoreType.DMA
    return pl.pallas_call(
        kernel,
        out_shape=jax.ShapeDtypeStruct((16, 384), BF16),
        in_specs=[hbm, hbm, hbm, hbm, hbm, hbm, hbm],
        out_specs=pl.BlockSpec(memory_space=pltpu.VMEM),
        scratch_shapes=[
            vmem((16, 384), BF16),
            vmem((2, 3, 64, 384), BF16),
            vmem((768, 1024), BF16),
            vmem((2, 512, 384), BF16),
            vmem((1, 1, 128), F32),
            vmem((16, 1, 128), F32),
            vmem((16, 128), BF16),
            vmem((256, 128), BF16),
            vmem((2, 256, 384), BF16),
            vmem((2, 128, 768), BF16),
            vmem((128, 256), BF16),
            vmem((2, 128, 768), BF16),
            vmem((2, 128, 1024), BF16),
            vmem((2, 7, 16, 1024), BF16),
            vmem((2, 2, 16, 1024), BF16),
            vmem((2, 128, 512), BF16),
            vmem((4, 4, 2, 16, 384), BF16),
            vmem((4, 3, 2, 16, 384), BF16),
            vmem((4, 2, 16, 384), BF16),
            vmem((8, 16, 384), BF16),
            pltpu.SMEM((2, 16), jnp.int32),
            dma((7,)),
            dma((4,)),
            dma((4,)),
            dma,
            dma,
            dma,
            dma((4, 2)),
            dma,
            dma((4,)),
            dma,
            dma((4,)),
            dma((4,)),
            dma,
            dma((2, 7)),
            dma,
            dma((2,)),
            dma,
            dma((4,)),
            dma,
            dma,
            pltpu.SemaphoreType.REGULAR((2,)),
        ],
        compiler_params=pltpu.CompilerParams(
            collective_id=0, has_side_effects=True, vmem_limit_bytes=60 << 20
        ),
        cost_estimate=pl.CostEstimate(flops=604_000_000, bytes_accessed=1_400_000, transcendentals=16384),
        name="modulated_feed_forward",
    )(tokens, token_frame, noise_level, jnp.transpose(modulation, (1, 0, 2)), gate_weight, up_weight, down_weight)


def solution(mesh):
    placed = (
        P("col", "row"),
        P("col"),
        P(),
        P(None, None, "row"),
        P("row", "col"),
        P("row", "col"),
        P("col", "row"),
    )
    return jax.shard_map(
        on_device, mesh=mesh, in_specs=placed, out_specs=P("col", "row"), check_vma=False
    )
```
